256 devices in a mesh: fsdp: 64 (over z, x, core), dp: 4 (over y).
Axes of the slice: x: 4, y: 4, z: 8, core: 2. Of those that a mesh axis runs over, the one named last changes fastest.
Arguments:
- grad: float32 [8192, 8192], P(('dp', 'fsdp')), parts along dimension 0, may hold values from -6 to 6
- moment: float32 [8192, 8192], P(('dp', 'fsdp')), parts along dimension 0, may hold values from -6 to 6
- second: float32 [8192, 8192], P('dp', 'fsdp'), parts along dimension 0, may hold values from 0.05 to 2
- left_basis: bfloat16 [8, 1024, 1024], P('dp', 'fsdp'), parts along dimension 0, may hold values from -0.1875 to 0.1875
- right_basis: bfloat16 [32, 1024, 1024], P('dp', 'fsdp'), parts along dimension 0, may hold values from -0.1875 to 0.1875
Outputs:
- update: float32 [8192, 8192], P(('dp', 'fsdp')), parts along dimension 0
- moment_new: float32 [8192, 8192], P(('dp', 'fsdp')), parts along dimension 0
- second_new: float32 [8192, 8192], P('dp', 'fsdp'), parts along dimension 0
The draws below stay inside these ranges and needn't reach their ends.
There are 4 independent parts, one for each index of `dp`. The reference program is written for one: setup_inputs(seed, part) draws one part's arguments, and reference() takes and returns one part's arrays. A program takes and returns all parts, laid end to end along the dimension named above; each array names one. Nothing has to cross between parts.
All inputs are finite; a program needn't handle non-finite values.
Results may differ from the reference program's by a relative error of at most 0.0045.
Values may be sent and summed in bfloat16 or wider, within the bound.
A program may use at most 128 MiB of HBM per device.

```python
import math
import jax
import jax.numpy as jnp
from jax import lax

B = 1024
R = 2048
RBLK = 8
LBLK = 2
C = 8192


def block_scale(own_key, extent, split, least, largest):
    def one(position, shards_of):
        heights = jax.random.uniform(jax.random.fold_in(jax.random.fold_in(own_key, 6), position), (shards_of,), jnp.float32, least / len(split), largest / len(split))
        return jnp.repeat(jnp.exp(heights), extent[position] // shards_of).reshape((-1,) + (1,) * (len(extent) - position - 1))

    gain = one(*split[0])
    for cut in split[1:]:
        gain = gain * one(*cut)
    return gain


def noise(key, extent, spread, most, cuts=(), held_as=jnp.bfloat16):
    drawn = spread * jax.random.normal(key, extent, jnp.float32)
    if cuts:
        drawn = drawn * block_scale(key, extent, cuts, -0.22, 0.18)
    return jnp.clip(drawn, -most, most).astype(held_as)


def setup_inputs(seed: int = 0, part: int = 0) -> dict:
    key_of = jax.random.split(jax.random.key(seed), 6)
    part_splits = jax.random.split(jax.random.fold_in(key_of[5], part), 6)
    return {
        "grad": noise(part_splits[0], (R, C), 1.0, 6.0, ((0, 64),), jnp.float32),
        "moment": noise(part_splits[1], (R, C), 1.0, 6.0, ((0, 64),), jnp.float32),
        "second": jnp.clip(jnp.exp(math.log(2.0) - 3.6888794 * jax.random.uniform(part_splits[2], (R, C), jnp.float32) ** block_scale(part_splits[2], (R, C), ((1, 64),), -0.2, 0.2)), 0.05, 2.0),
        "left_basis": noise(part_splits[3], (LBLK, B, B), B ** -0.5, 0.1875, ((1, 64),)),
        "right_basis": noise(part_splits[4], (RBLK, B, B), B ** -0.5, 0.1875, ((1, 64),)),
    }


BETA_ONE = 0.9
BETA_TWO = 0.95
EPSILON = 1e-08

def round_keep(value):
    return lax.optimization_barrier(value.astype(jnp.bfloat16)).astype(jnp.float32)

def reference(grad, moment, second, left_basis, right_basis):
    highest = lax.Precision.HIGHEST
    lblocks = R // B
    cols = RBLK * B
    moment_new = BETA_ONE * moment + (1.0 - BETA_ONE) * grad
    packed = round_keep(jnp.stack([grad, moment_new]))
    right_full = right_basis.astype(jnp.float32)
    left_full = left_basis.astype(jnp.float32)
    turned = jnp.einsum('xrkb,kbi->xrki', packed.reshape(2, R, RBLK, B), right_full, precision=highest)
    turned = round_keep(turned)
    projected = jnp.einsum('xlkc,lki->xlic', turned.reshape(2, lblocks, B, cols), left_full, precision=highest)
    projected = projected.reshape(2, R, cols)
    grad_eigen = projected[0]
    moment_eigen = projected[1]
    second_new = BETA_TWO * second + (1.0 - BETA_TWO) * grad_eigen * grad_eigen
    scaled = round_keep(moment_eigen / (jnp.sqrt(second_new) + EPSILON))
    back_left = jnp.einsum('lki,lic->lkc', left_full, scaled.reshape(lblocks, B, cols), precision=highest)
    back_left = round_keep(back_left)
    update = jnp.einsum('rki,kbi->rkb', back_left.reshape(R, RBLK, B), right_full, precision=highest)
    return (update.reshape(R, cols), moment_new, second_new)
```

```python
import jax
import jax.numpy as jnp
from jax import lax
from jax.experimental import pallas as pl
from jax.experimental.pallas import tpu as pltpu
from jax.sharding import PartitionSpec as P

BETA_ONE = 0.9
BETA_TWO = 0.95
EPSILON = 1e-08

NZ, NX, NC = 8, 4, 2
NP = NX * NC
F32, BF16 = jnp.float32, jnp.bfloat16


def kernel(
    grad, moment, second, left, right,
    upd_o, mom_o, sec_o,
    gv, mv, sv, ps, pr, rb, tb, cb, lb, sc, bk, wb, ub,
    in_sem, out_sem,
    rz_s, rz_r, rx_s, rx_r, rd_s, rd_r,
    lz_s, lz_r, lx_s, lx_r, lo_s, lo_r, ld_s, ld_r,
    pz_s, pz_r, tx_s, tx_r, bx_s, bx_r, uz_s, uz_r,
):
    f = lax.axis_index("fsdp")
    z, p = f // NP, lax.rem(f, NP)
    x, c = p // NC, lax.rem(p, NC)
    row = gv.shape[0]
    width = rb.shape[-1]

    def dev(zz, xx, cc):
        return {"fsdp": (zz * NX + xx) * NC + cc}

    def up(v, d, n):
        return lax.rem(v + d + 2 * n, n)

    def zdev(d):
        return dev(up(z, d, NZ), x, c)

    def xdev(d):
        return dev(z, up(x, d, NX), c)

    other = dev(z, x, 1 - c)

    def remote(src, dst, ss, rs, to):
        return pltpu.make_async_remote_copy(
            src_ref=src, dst_ref=dst, send_sem=ss, recv_sem=rs, device_id=to, device_id_type=pl.DeviceIdType.MESH
        )

    def wait(ref, sem):
        pltpu.make_async_copy(ref, ref, sem).wait()

    loads = [
        pltpu.make_async_copy(grad, gv, in_sem.at[0]),
        pltpu.make_async_copy(moment, mv, in_sem.at[1]),
        pltpu.make_async_copy(second, sv, in_sem.at[2]),
        pltpu.make_async_copy(left, lb.at[:, z, x, c], in_sem.at[3]),
        pltpu.make_async_copy(right.at[z], rb.at[z, x, c], in_sem.at[4]),
    ]
    for load in loads:
        load.start()

    barrier = pltpu.get_barrier_semaphore()

    def greet(d, carry):
        pl.semaphore_signal(barrier, inc=1, device_id=zdev(d), device_id_type=pl.DeviceIdType.MESH)
        pl.semaphore_signal(
            barrier, inc=1, device_id={"fsdp": z * NP + lax.rem(p + d, NP)}, device_id_type=pl.DeviceIdType.MESH
        )
        return carry

    lax.fori_loop(1, NZ, greet, 0)

    loads[0].wait()
    loads[1].wait()

    def pack(k, carry):
        cols = pl.ds(pl.multiple_of(k * width, width), width)
        g = gv[:, cols]
        m = BETA_ONE * mv[:, cols] + (1.0 - BETA_ONE) * g
        mv[:, cols] = m
        ps[k, 0:row] = g.astype(BF16)
        ps[k, row : 2 * row] = m.astype(BF16)
        return carry

    lax.fori_loop(0, NZ, pack, 0)
    store_m = pltpu.make_async_copy(mv, mom_o, out_sem.at[0])
    store_m.start()
    pr[z] = ps[z]
    loads[3].wait()
    loads[4].wait()

    pl.semaphore_wait(barrier, 2 * (NZ - 1))

    def right_z(d, carry):
        k = up(z, d, NZ)
        remote(right.at[k], rb.at[z, x, c], rz_s, rz_r, zdev(d)).start()
        return carry

    lax.fori_loop(1, NZ, right_z, 0)

    def left_z(s, way, half=False):
        sign = 1 if way == 0 else -1
        blk = up(z, -sign * (s - 1), NZ)
        if half:
            ref = lb.at[way, blk, x, c]
        else:
            ref = lb.at[:, blk, x, c]
        return remote(ref, ref, lz_s.at[s, way], lz_r.at[s, way], zdev(sign))

    for way in range(2):
        left_z(1, way).start()

    def packed_z(i, carry):
        d = (i + 2) // 2
        off = jnp.where(lax.rem(i, 2) == 0, d, -d)
        k = up(z, off, NZ)
        remote(ps.at[k], pr.at[z], pz_s, pz_r.at[z], dev(k, x, c)).start()
        return carry

    lax.fori_loop(0, NZ - 1, packed_z, 0)

    def right_x(way):
        ref = rb.at[:, x, c]
        return remote(ref, ref, rx_s.at[way], rx_r.at[way], xdev(1 if way == 0 else -1))

    def right_half(way):
        ref = rb.at[pl.ds(way * (NZ // 2), NZ // 2), up(x, -1 if way == 0 else 1, NX), c]
        return remote(ref, ref, rx_s.at[2 + way], rx_r.at[2 + way], xdev(1 if way == 0 else -1))

    def right_core(xx, i):
        ref = rb.at[:, xx, c]
        return remote(ref, ref, rd_s.at[i], rd_r.at[i], other)

    def left_x(zz, way):
        ref = lb.at[:, zz, x, c]
        return remote(ref, ref, lx_s.at[zz, way], lx_r.at[zz, way], xdev(1 if way == 0 else -1))

    def left_half(zz, way):
        ref = lb.at[way, zz, up(x, -1 if way == 0 else 1, NX), c]
        return remote(ref, ref, lo_s.at[zz, way], lo_r.at[zz, way], xdev(1 if way == 0 else -1))

    def left_core(zz):
        ref = lb.at[:, zz, :, c]
        return remote(ref, ref, ld_s.at[zz], ld_r.at[zz], other)

    def blocks(s):
        if s == 0 or s == NZ // 2:
            return [up(z, s, NZ)]
        return [up(z, -s, NZ), up(z, s, NZ)]

    def stage(s):
        if 1 <= s <= NZ // 2:
            for way in range(2):
                left_z(s, way, half=s == NZ // 2).wait_recv()
                if s < NZ // 2:
                    left_z(s + 1, way, half=s + 1 == NZ // 2).start()
        if s <= NZ // 2:
            for zz in blocks(s):
                for way in range(2):
                    left_x(zz, way).start()
        if 1 <= s <= NZ // 2 + 1:
            for zz in blocks(s - 1):
                for way in range(2):
                    left_x(zz, way).wait_recv()
                    left_half(zz, way).start()
        if 2 <= s <= NZ // 2 + 2:
            for zz in blocks(s - 2):
                for way in range(2):
                    left_half(zz, way).wait_recv()
                left_core(zz).start()

    wait(right.at[pl.ds(0, NZ - 1)], rz_r)
    for way in range(2):
        right_x(way).start()
    right_core(x, 0).start()
    stage(0)
    for way in range(2):
        right_x(way).wait_recv()
        right_half(way).start()
        right_core(up(x, -1 if way == 0 else 1, NX), 1 + way).start()
    stage(1)
    for way in range(2):
        right_half(way).wait_recv()
    right_core(up(x, 2, NX), 3).start()
    stage(2)
    for i in range(4):
        right_core(x, i).wait_recv()

    def turn(i, carry):
        d = (i + 1) // 2
        zz = up(z, jnp.where(lax.rem(i, 2) == 1, -d, d), NZ)

        @pl.when(i > 0)
        def _():
            wait(pr.at[zz], pz_r.at[zz])

        t = jnp.dot(pr[zz], rb[...].reshape(width, width), preferred_element_type=F32).astype(BF16)
        seg = width // NP
        for q in range(NP):
            tb[zz, q, :, 0:seg] = t[0:row, q * seg : (q + 1) * seg]
            tb[zz, q, :, seg : 2 * seg] = t[row : 2 * row, q * seg : (q + 1) * seg]
        cb[zz, p] = tb[zz, p]

        def send(e, carry):
            q = lax.rem(p + e, NP)
            remote(tb.at[zz, q], cb.at[zz, p], tx_s, tx_r, {"fsdp": z * NP + q}).start()
            return carry

        lax.fori_loop(1, NP, send, 0)
        return carry

    lax.fori_loop(0, 3, turn, 0)
    stage(3)
    lax.fori_loop(3, 5, turn, 0)
    stage(4)
    lax.fori_loop(5, 7, turn, 0)
    stage(5)
    lax.fori_loop(7, 8, turn, 0)
    stage(6)

    def left_done(zz, carry):
        left_core(zz).wait_recv()
        return carry

    lax.fori_loop(0, NZ, left_done, 0)
    wait(cb.at[pl.ds(0, NZ - 1)], tx_r)
    loads[2].wait()

    seg = width // NP
    part = width // 4

    def project(i, carry):
        l, q = i // 4, lax.rem(i, 4)
        cols = pl.ds(pl.multiple_of(q * part, part), part)
        basis = lb[l, :, :, :, :, cols].reshape(width, part)
        turned = cb[pl.ds(l * (NZ // 2), NZ // 2)].reshape(width, 2 * seg)
        both = lax.dot_general(basis, turned, (((0,), (0,)), ((), ())), preferred_element_type=F32)
        g, m = both[:, :seg], both[:, seg:]
        rows = pl.ds(pl.multiple_of(i * part, part), part)
        s = BETA_TWO * sv[rows, :] + (1.0 - BETA_TWO) * g * g
        sv[rows, :] = s
        sc[rows, :] = (m / (jnp.sqrt(s) + EPSILON)).astype(BF16)
        return carry

    lax.fori_loop(0, 8, project, 0)
    store_s = pltpu.make_async_copy(sv, sec_o, out_sem.at[1])
    store_s.start()

    def far(i):
        d = (NZ - i) // 2
        return up(z, jnp.where(lax.rem(i, 2) == 1, d, -d), NZ)

    def back(i, carry):
        zz = far(i)
        l, q = zz // 4, lax.rem(zz, 4)
        basis = lb[l, pl.ds(2 * q, 2)].reshape(NP * row, width)
        scaled = sc[pl.ds(pl.multiple_of(l * width, width), width), :]
        out = jnp.dot(basis, scaled, preferred_element_type=F32).astype(BF16)
        bk[zz] = out.reshape(NP, row, seg)
        wb[zz, p] = bk[zz, p]

        def send(e, carry):
            q = lax.rem(p + e, NP)
            remote(bk.at[zz, q], wb.at[zz, p], bx_s, bx_r.at[zz], {"fsdp": z * NP + q}).start()
            return carry

        lax.fori_loop(1, NP, send, 0)
        return carry

    lax.fori_loop(0, NZ, back, 0)

    mine = pl.ds(pl.multiple_of(z * width, width), width)

    def update(i, carry):
        zz = far(i)
        wait(wb.at[zz, pl.ds(0, NP - 1)], bx_r.at[zz])
        rows = jnp.concatenate([wb[zz, q] for q in range(NP)], axis=1)
        out = lax.dot_general(
            rows, rb[...].reshape(width, width), (((1,), (1,)), ((), ())), preferred_element_type=F32
        )
        ub[zz] = out.astype(BF16)

        @pl.when(i < NZ - 1)
        def _():
            remote(ub.at[zz], upd_o.at[:, mine], uz_s, uz_r, dev(zz, x, c)).start()

        return carry

    lax.fori_loop(0, NZ, update, 0)
    store_u = pltpu.make_async_copy(ub.at[z], upd_o.at[:, mine], out_sem.at[2])
    store_u.start()

    for way in range(2):
        right_x(way).wait_send()
        right_half(way).wait_send()
        for s in range(1, NZ // 2 + 1):
            left_z(s, way, half=s == NZ // 2).wait_send()
    for i in range(4):
        right_core(x, i).wait_send()

    def drain(zz, carry):
        for way in range(2):
            left_x(zz, way).wait_send()
            left_half(zz, way).wait_send()
        left_core(zz).wait_send()
        return carry

    lax.fori_loop(0, NZ, drain, 0)
    wait(right.at[pl.ds(0, NZ - 1)], rz_s)
    wait(ps.at[pl.ds(0, NZ - 1)], pz_s)
    wait(tb.at[pl.ds(0, NZ - 1)], tx_s)
    wait(bk.at[pl.ds(0, NZ - 1)], bx_s)
    wait(ub.at[pl.ds(0, NZ - 1)], uz_s)
    wait(ub.at[pl.ds(0, NZ - 1)], uz_r)
    store_m.wait()
    store_s.wait()
    store_u.wait()


def local(grad, moment, second, left_basis, right_basis):
    row, cols = grad.shape
    lblocks, piece, width = left_basis.shape
    total, seg = second.shape
    any_spec = pl.BlockSpec(memory_space=pl.ANY)
    dma = pltpu.SemaphoreType.DMA
    update, moment_new, second_new = pl.pallas_call(
        kernel,
        out_shape=(
            jax.ShapeDtypeStruct((row, cols), BF16),
            jax.ShapeDtypeStruct((row, cols), F32),
            jax.ShapeDtypeStruct((total, seg), F32),
        ),
        in_specs=[any_spec] * 5,
        out_specs=[any_spec] * 3,
        scratch_shapes=[
            pltpu.VMEM((row, cols), F32),
            pltpu.VMEM((row, cols), F32),
            pltpu.VMEM((total, seg), F32),
            pltpu.VMEM((NZ, 2 * row, width), BF16),
            pltpu.VMEM((NZ, 2 * row, width), BF16),
            pltpu.VMEM((NZ, NX, NC, piece, width), BF16),
            pltpu.VMEM((NZ, NP, row, 2 * seg), BF16),
            pltpu.VMEM((NZ, NP, row, 2 * seg), BF16),
            pltpu.VMEM((lblocks, NZ, NX, NC, piece, width), BF16),
            pltpu.VMEM((total, seg), BF16),
            pltpu.VMEM((NZ, NP, row, seg), BF16),
            pltpu.VMEM((NZ, NP, row, seg), BF16),
            pltpu.VMEM((NZ, row, width), BF16),
            dma((5,)), dma((3,)),
            dma, dma, dma((4,)), dma((4,)), dma((4,)), dma((4,)),
            dma((5, 2)), dma((5, 2)), dma((NZ, 2)), dma((NZ, 2)), dma((NZ, 2)), dma((NZ, 2)), dma((NZ,)), dma((NZ,)),
            dma, dma((NZ,)), dma, dma, dma, dma((NZ,)), dma, dma,
        ],
        compiler_params=pltpu.CompilerParams(
            collective_id=0, has_side_effects=True, vmem_limit_bytes=40 * 2**20
        ),
        cost_estimate=pl.CostEstimate(flops=3 * 2**30, bytes_accessed=8 * 2**20, transcendentals=2**19),
        name="soap_step",
    )(grad, moment, second, left_basis, right_basis)
    return update.astype(F32), moment_new, second_new


def solution(mesh):
    in_specs = (
        P(("dp", "fsdp"), None),
        P(("dp", "fsdp"), None),
        P("dp", "fsdp"),
        P("dp", "fsdp", None),
        P("dp", "fsdp", None),
    )
    out_specs = (P(("dp", "fsdp"), None), P(("dp", "fsdp"), None), P("dp", "fsdp"))
    return jax.shard_map(local, mesh=mesh, in_specs=in_specs, out_specs=out_specs, check_vma=False)
```

```python
import jax
import jax.numpy as jnp
from jax import lax
from jax.experimental import pallas as pl
from jax.experimental.pallas import tpu as pltpu
from jax.sharding import PartitionSpec as P

BETA_ONE = 0.9
BETA_TWO = 0.95
EPSILON = 1e-08

NZ, NX, NC = 8, 4, 2
NP = NX * NC
F32, BF16 = jnp.float32, jnp.bfloat16


def kernel(
    grad, moment, second, left, right,
    upd_o, mom_o, sec_o,
    gv, mv, sv, ps, pr, rb, tb, cb, lb, sc, bk, wb, ub,
    in_sem, out_sem,
    rz_s, rz_r, rx_s, rx_r, rd_s, rd_r,
    lz_s, lz_r, lx_s, lx_r, lo_s, lo_r, ld_s, ld_r,
    pz_s, pz_r, tx_s, tx_r, bx_s, bx_r, uz_s, uz_r,
):
    f = lax.axis_index("fsdp")
    z, p = f // NP, lax.rem(f, NP)
    x, c = p // NC, lax.rem(p, NC)
    row = gv.shape[0]
    width = rb.shape[-1]

    def dev(zz, xx, cc):
        return {"fsdp": (zz * NX + xx) * NC + cc}

    def up(v, d, n):
        return lax.rem(v + d + 2 * n, n)

    def zdev(d):
        return dev(up(z, d, NZ), x, c)

    def xdev(d):
        return dev(z, up(x, d, NX), c)

    other = dev(z, x, 1 - c)

    def remote(src, dst, ss, rs, to):
        return pltpu.make_async_remote_copy(
            src_ref=src, dst_ref=dst, send_sem=ss, recv_sem=rs, device_id=to, device_id_type=pl.DeviceIdType.MESH
        )

    def wait(ref, sem):
        pltpu.make_async_copy(ref, ref, sem).wait()

    loads = [
        pltpu.make_async_copy(grad, gv, in_sem.at[0]),
        pltpu.make_async_copy(moment, mv, in_sem.at[1]),
        pltpu.make_async_copy(second, sv, in_sem.at[2]),
        pltpu.make_async_copy(left, lb.at[:, z, x, c], in_sem.at[3]),
        pltpu.make_async_copy(right.at[z], rb.at[z, x, c], in_sem.at[4]),
    ]
    for load in loads:
        load.start()

    barrier = pltpu.get_barrier_semaphore()

    def greet(d, carry):
        pl.semaphore_signal(barrier, inc=1, device_id=zdev(d), device_id_type=pl.DeviceIdType.MESH)
        pl.semaphore_signal(
            barrier, inc=1, device_id={"fsdp": z * NP + lax.rem(p + d, NP)}, device_id_type=pl.DeviceIdType.MESH
        )
        return carry

    lax.fori_loop(1, NZ, greet, 0)

    loads[0].wait()
    loads[1].wait()

    def pack(k, carry):
        cols = pl.ds(pl.multiple_of(k * width, width), width)
        g = gv[:, cols]
        m = BETA_ONE * mv[:, cols] + (1.0 - BETA_ONE) * g
        mv[:, cols] = m
        ps[k, 0:row] = g.astype(BF16)
        ps[k, row : 2 * row] = m.astype(BF16)
        return carry

    lax.fori_loop(0, NZ, pack, 0)
    store_m = pltpu.make_async_copy(mv, mom_o, out_sem.at[0])
    store_m.start()
    pr[z] = ps[z]
    loads[3].wait()
    loads[4].wait()

    pl.semaphore_wait(barrier, 2 * (NZ - 1))

    def right_z(d, carry):
        k = up(z, d, NZ)
        remote(right.at[k], rb.at[z, x, c], rz_s, rz_r, zdev(d)).start()
        return carry

    def left_z(step, way):
        sign = 1 if way == 0 else -1
        blk = z if step < 2 else up(z, -2 * sign, NZ)
        ref = lb.at[way, blk, x, c] if step == 3 else lb.at[:, blk, x, c]
        return remote(ref, ref, lz_s.at[step, way], lz_r.at[step, way], zdev((1, 2, 1, 2)[step] * sign))

    def packed_z(d):
        k = up(z, d, NZ)
        remote(ps.at[k], pr.at[z], pz_s, pz_r.at[z], dev(k, x, c)).start()

    def right_x(way):
        ref = rb.at[:, x, c]
        return remote(ref, ref, rx_s.at[way], rx_r.at[way], xdev(1 if way == 0 else -1))

    def right_half(way):
        ref = rb.at[pl.ds(way * (NZ // 2), NZ // 2), up(x, -1 if way == 0 else 1, NX), c]
        return remote(ref, ref, rx_s.at[2 + way], rx_r.at[2 + way], xdev(1 if way == 0 else -1))

    def right_core(xx, i):
        ref = rb.at[:, xx, c]
        return remote(ref, ref, rd_s.at[i], rd_r.at[i], other)

    def left_x(zz, way):
        ref = lb.at[:, zz, x, c]
        return remote(ref, ref, lx_s.at[zz, way], lx_r.at[zz, way], xdev(1 if way == 0 else -1))

    def left_half(zz, way):
        ref = lb.at[way, zz, up(x, -1 if way == 0 else 1, NX), c]
        return remote(ref, ref, lo_s.at[zz, way], lo_r.at[zz, way], xdev(1 if way == 0 else -1))

    def left_core(zz):
        ref = lb.at[:, zz, :, c]
        return remote(ref, ref, ld_s.at[zz], ld_r.at[zz], other)

    def near(d):
        return [up(z, -d, NZ), up(z, d, NZ)]

    def left_send(group):
        for zz in group:
            for way in range(2):
                left_x(zz, way).start()

    def left_pass(group):
        for zz in group:
            for way in range(2):
                left_x(zz, way).wait_recv()
                left_half(zz, way).start()

    def left_share(group):
        for zz in group:
            for way in range(2):
                left_half(zz, way).wait_recv()
            left_core(zz).start()

    own, two, last = [z], near(2), near(3) + [up(z, 4, NZ)]

    for way in range(2):
        left_z(0, way).start()
    left_send(own)
    lax.fori_loop(1, NZ, right_z, 0)
    for way in range(2):
        left_z(1, way).start()
    packed_z(1)
    packed_z(-1)

    for way in range(2):
        left_z(0, way).wait_recv()
    left_send(near(1))
    left_pass(own)

    wait(right.at[pl.ds(0, NZ - 1)], rz_r)
    for way in range(2):
        right_x(way).start()
    right_core(x, 0).start()

    for way in range(2):
        left_z(1, way).wait_recv()
        left_z(2, way).start()
        left_z(3, way).start()
    packed_z(3)
    packed_z(-3)
    left_send(two)
    left_pass(near(1))
    left_share(own)

    for way in range(2):
        right_x(way).wait_recv()
        right_half(way).start()
        right_core(up(x, -1 if way == 0 else 1, NX), 1 + way).start()

    for way in range(2):
        left_z(2, way).wait_recv()
        left_z(3, way).wait_recv()
    for d in (4, 2, -2):
        packed_z(d)
    left_send(last)
    left_pass(two)
    left_share(near(1))

    for way in range(2):
        right_half(way).wait_recv()
    right_core(up(x, 2, NX), 3).start()
    for i in range(4):
        right_core(x, i).wait_recv()

    def turn(i, carry):
        d = jnp.where(i < 3, (i + 1) // 2, jnp.where(i < 5, 3, jnp.where(i == 5, 4, 2)))
        odd = jnp.where(i > 5, lax.rem(i + 1, 2), lax.rem(i, 2))
        zz = up(z, jnp.where(odd == 1, -d, d), NZ)

        @pl.when(i > 0)
        def _():
            wait(pr.at[zz], pz_r.at[zz])

        t = jnp.dot(pr[zz], rb[...].reshape(width, width), preferred_element_type=F32).astype(BF16)
        seg = width // NP
        for q in range(NP):
            tb[zz, q, :, 0:seg] = t[0:row, q * seg : (q + 1) * seg]
            tb[zz, q, :, seg : 2 * seg] = t[row : 2 * row, q * seg : (q + 1) * seg]
        cb[zz, p] = tb[zz, p]

        def send(e, carry):
            q = lax.rem(p + e, NP)
            remote(tb.at[zz, q], cb.at[zz, p], tx_s, tx_r, {"fsdp": z * NP + q}).start()
            return carry

        lax.fori_loop(1, NP, send, 0)
        return carry

    lax.fori_loop(0, 3, turn, 0)
    left_pass(last)
    left_share(two)
    lax.fori_loop(3, 5, turn, 0)
    left_share(last)
    lax.fori_loop(5, 8, turn, 0)

    def left_done(zz, carry):
        left_core(zz).wait_recv()
        return carry

    lax.fori_loop(0, NZ, left_done, 0)
    wait(cb.at[pl.ds(0, NZ - 1)], tx_r)
    loads[2].wait()

    seg = width // NP
    part = width // 4

    def project(i, carry):
        l, q = i // 4, lax.rem(i, 4)
        cols = pl.ds(pl.multiple_of(q * part, part), part)
        basis = lb[l, :, :, :, :, cols].reshape(width, part)
        turned = cb[pl.ds(l * (NZ // 2), NZ // 2)].reshape(width, 2 * seg)
        both = lax.dot_general(basis, turned, (((0,), (0,)), ((), ())), preferred_element_type=F32)
        g, m = both[:, :seg], both[:, seg:]
        rows = pl.ds(pl.multiple_of(i * part, part), part)
        s = BETA_TWO * sv[rows, :] + (1.0 - BETA_TWO) * g * g
        sv[rows, :] = s
        sc[rows, :] = (m / (jnp.sqrt(s) + EPSILON)).astype(BF16)
        return carry

    lax.fori_loop(0, 8, project, 0)
    store_s = pltpu.make_async_copy(sv, sec_o, out_sem.at[1])
    store_s.start()

    def far(i):
        d = (NZ - i) // 2
        return up(z, jnp.where(lax.rem(i, 2) == 1, d, -d), NZ)

    def back(i, carry):
        zz = far(i)
        l, q = zz // 4, lax.rem(zz, 4)
        basis = lb[l, pl.ds(2 * q, 2)].reshape(NP * row, width)
        scaled = sc[pl.ds(pl.multiple_of(l * width, width), width), :]
        out = jnp.dot(basis, scaled, preferred_element_type=F32).astype(BF16)
        bk[zz] = out.reshape(NP, row, seg)
        wb[zz, p] = bk[zz, p]

        def send(e, carry):
            q = lax.rem(p + e, NP)
            remote(bk.at[zz, q], wb.at[zz, p], bx_s, bx_r.at[zz], {"fsdp": z * NP + q}).start()
            return carry

        lax.fori_loop(1, NP, send, 0)
        return carry

    lax.fori_loop(0, NZ, back, 0)

    mine = pl.ds(pl.multiple_of(z * width, width), width)

    def update(i, carry):
        zz = far(i)
        wait(wb.at[zz, pl.ds(0, NP - 1)], bx_r.at[zz])
        rows = jnp.concatenate([wb[zz, q] for q in range(NP)], axis=1)
        out = lax.dot_general(
            rows, rb[...].reshape(width, width), (((1,), (1,)), ((), ())), preferred_element_type=F32
        )
        ub[zz] = out.astype(BF16)

        @pl.when(i < NZ - 1)
        def _():
            remote(ub.at[zz], upd_o.at[:, mine], uz_s, uz_r, dev(zz, x, c)).start()

        return carry

    lax.fori_loop(0, NZ, update, 0)
    store_u = pltpu.make_async_copy(ub.at[z], upd_o.at[:, mine], out_sem.at[2])
    store_u.start()

    for way in range(2):
        right_x(way).wait_send()
        right_half(way).wait_send()
        for step in range(4):
            left_z(step, way).wait_send()
    for i in range(4):
        right_core(x, i).wait_send()

    def drain(zz, carry):
        for way in range(2):
            left_x(zz, way).wait_send()
            left_half(zz, way).wait_send()
        left_core(zz).wait_send()
        return carry

    lax.fori_loop(0, NZ, drain, 0)
    wait(right.at[pl.ds(0, NZ - 1)], rz_s)
    wait(ps.at[pl.ds(0, NZ - 1)], pz_s)
    wait(tb.at[pl.ds(0, NZ - 1)], tx_s)
    wait(bk.at[pl.ds(0, NZ - 1)], bx_s)
    wait(ub.at[pl.ds(0, NZ - 1)], uz_s)
    wait(ub.at[pl.ds(0, NZ - 1)], uz_r)
    store_m.wait()
    store_s.wait()
    store_u.wait()


def local(grad, moment, second, left_basis, right_basis):
    row, cols = grad.shape
    lblocks, piece, width = left_basis.shape
    total, seg = second.shape
    any_spec = pl.BlockSpec(memory_space=pl.ANY)
    dma = pltpu.SemaphoreType.DMA
    update, moment_new, second_new = pl.pallas_call(
        kernel,
        out_shape=(
            jax.ShapeDtypeStruct((row, cols), BF16),
            jax.ShapeDtypeStruct((row, cols), F32),
            jax.ShapeDtypeStruct((total, seg), F32),
        ),
        in_specs=[any_spec] * 5,
        out_specs=[any_spec] * 3,
        scratch_shapes=[
            pltpu.VMEM((row, cols), F32),
            pltpu.VMEM((row, cols), F32),
            pltpu.VMEM((total, seg), F32),
            pltpu.VMEM((NZ, 2 * row, width), BF16),
            pltpu.VMEM((NZ, 2 * row, width), BF16),
            pltpu.VMEM((NZ, NX, NC, piece, width), BF16),
            pltpu.VMEM((NZ, NP, row, 2 * seg), BF16),
            pltpu.VMEM((NZ, NP, row, 2 * seg), BF16),
            pltpu.VMEM((lblocks, NZ, NX, NC, piece, width), BF16),
            pltpu.VMEM((total, seg), BF16),
            pltpu.VMEM((NZ, NP, row, seg), BF16),
            pltpu.VMEM((NZ, NP, row, seg), BF16),
            pltpu.VMEM((NZ, row, width), BF16),
            dma((5,)), dma((3,)),
            dma, dma, dma((4,)), dma((4,)), dma((4,)), dma((4,)),
            dma((4, 2)), dma((4, 2)), dma((NZ, 2)), dma((NZ, 2)), dma((NZ, 2)), dma((NZ, 2)), dma((NZ,)), dma((NZ,)),
            dma, dma((NZ,)), dma, dma, dma, dma((NZ,)), dma, dma,
        ],
        compiler_params=pltpu.CompilerParams(
            collective_id=0, has_side_effects=True, vmem_limit_bytes=62 * 2**20
        ),
        cost_estimate=pl.CostEstimate(flops=3 * 2**30, bytes_accessed=8 * 2**20, transcendentals=2**19),
        name="soap_step",
    )(grad, moment, second, left_basis, right_basis)
    return update.astype(F32), moment_new, second_new


def solution(mesh):
    in_specs = (
        P(("dp", "fsdp"), None),
        P(("dp", "fsdp"), None),
        P("dp", "fsdp"),
        P("dp", "fsdp", None),
        P("dp", "fsdp", None),
    )
    out_specs = (P(("dp", "fsdp"), None), P(("dp", "fsdp"), None), P("dp", "fsdp"))
    return jax.shard_map(local, mesh=mesh, in_specs=in_specs, out_specs=out_specs, check_vma=False)
```

```python
import jax
import jax.numpy as jnp
from jax import lax
from jax.experimental import pallas as pl
from jax.experimental.pallas import tpu as pltpu
from jax.sharding import PartitionSpec as P

BETA_ONE = 0.9
BETA_TWO = 0.95
EPSILON = 1e-08

NZ, NX, NC = 8, 4, 2
NP = NX * NC
F32, BF16 = jnp.float32, jnp.bfloat16

FILL = (1, -1)
REST = (2, -2, 3, -3, 4)


def kernel(
    grad, moment, second, left, right,
    upd_o, mom_o, sec_o,
    gv, mv, sv, ps, pr, rb, tb, cb, lb, ac, sc, bk, wb, ub,
    in_sem, out_sem,
    rz_s, rz_r, rx_s, rx_r, rd_s, rd_r,
    lz_s, lz_r, lx_s, lx_r, lo_s, lo_r, ld_s, ld_r,
    pz_s, pz_r, tx_s, tx_r, bx_s, bx_r, uz_s, uz_r,
):
    f = lax.axis_index("fsdp")
    z, p = f // NP, lax.rem(f, NP)
    x, c = p // NC, lax.rem(p, NC)
    row = gv.shape[0]
    width = rb.shape[-1]

    def dev(zz, xx, cc):
        return {"fsdp": (zz * NX + xx) * NC + cc}

    def up(v, d, n):
        return lax.rem(v + d + 2 * n, n)

    def zdev(d):
        return dev(up(z, d, NZ), x, c)

    def xdev(d):
        return dev(z, up(x, d, NX), c)

    other = dev(z, x, 1 - c)

    def remote(src, dst, ss, rs, to):
        return pltpu.make_async_remote_copy(
            src_ref=src, dst_ref=dst, send_sem=ss, recv_sem=rs, device_id=to, device_id_type=pl.DeviceIdType.MESH
        )

    def wait(ref, sem):
        pltpu.make_async_copy(ref, ref, sem).wait()

    barrier = pltpu.get_barrier_semaphore()
    for d in (4, 3, -3, 2, -2, 1, -1):
        pl.semaphore_signal(barrier, inc=1, device_id=zdev(d), device_id_type=pl.DeviceIdType.MESH)
    for d in range(1, NP):
        to = {"fsdp": z * NP + lax.rem(p + d, NP)}
        pl.semaphore_signal(barrier, inc=1, device_id=to, device_id_type=pl.DeviceIdType.MESH)

    loads = [
        pltpu.make_async_copy(left, lb.at[:, z, x, c], in_sem.at[0]),
        pltpu.make_async_copy(right.at[z], rb.at[z, x, c], in_sem.at[1]),
        pltpu.make_async_copy(grad, gv, in_sem.at[2]),
        pltpu.make_async_copy(moment, mv, in_sem.at[3]),
        pltpu.make_async_copy(second, sv, in_sem.at[4]),
    ]
    for load in loads:
        load.start()
    ac[...] = jnp.zeros_like(ac)
    loads[0].wait()
    loads[1].wait()
    pl.semaphore_wait(barrier, 2 * (NZ - 1))

    def right_z(d):
        group = 0 if abs(d) <= 2 else 1
        remote(right.at[up(z, d, NZ)], rb.at[z, x, c], rz_s, rz_r.at[group], zdev(d)).start()

    def left_z(step, way):
        sign = 1 if way == 0 else -1
        blk = up(z, -(0, 1, 2, 2)[step] * sign, NZ)
        ref = lb.at[way, blk, x, c] if step == 3 else lb.at[:, blk, x, c]
        return remote(ref, ref, lz_s.at[step, way], lz_r.at[step, way], zdev((1, 1, 1, 2)[step] * sign))

    def packed_z(d):
        k = up(z, d, NZ)
        remote(ps.at[k], pr.at[z], pz_s, pz_r.at[z], dev(k, x, c)).start()

    def right_x(zz):
        ref = rb.at[zz, x, c]
        for way in range(2):
            remote(ref, ref, rx_s.at[way], rx_r.at[way], xdev(1 if way == 0 else -1)).start()

    def right_half(way):
        ref = rb.at[pl.ds(way * (NZ // 2), NZ // 2), up(x, -1 if way == 0 else 1, NX), c]
        return remote(ref, ref, rx_s.at[2 + way], rx_r.at[2 + way], xdev(1 if way == 0 else -1))

    def right_core(xx, i):
        ref = rb.at[:, xx, c]
        return remote(ref, ref, rd_s.at[i], rd_r.at[i], other)

    def left_x(zz, way):
        ref = lb.at[:, zz, x, c]
        return remote(ref, ref, lx_s.at[zz, way], lx_r.at[zz, way], xdev(1 if way == 0 else -1))

    def left_half(zz, way):
        ref = lb.at[way, zz, up(x, -1 if way == 0 else 1, NX), c]
        return remote(ref, ref, lo_s.at[zz, way], lo_r.at[zz, way], xdev(1 if way == 0 else -1))

    def left_core(zz):
        ref = lb.at[:, zz, :, c]
        return remote(ref, ref, ld_s.at[zz], ld_r.at[zz], other)

    def near(d):
        return [up(z, -d, NZ), up(z, d, NZ)]

    def left_send(group):
        for zz in group:
            for way in range(2):
                left_x(zz, way).start()

    def left_pass(group):
        for zz in group:
            for way in range(2):
                left_x(zz, way).wait_recv()
                left_half(zz, way).start()

    def left_share(group):
        for zz in group:
            for way in range(2):
                left_half(zz, way).wait_recv()
            left_core(zz).start()

    own, two, last = [z], near(2), near(3) + [up(z, 4, NZ)]

    for way in range(2):
        left_z(0, way).start()
    left_send(own)
    right_x(z)
    for d in (1, -1, 2, -2, 3, -3, 4):
        right_z(d)

    loads[2].wait()
    loads[3].wait()

    def pack(k, carry):
        cols = pl.ds(pl.multiple_of(k * width, width), width)
        g = gv[:, cols]
        m = BETA_ONE * mv[:, cols] + (1.0 - BETA_ONE) * g
        mv[:, cols] = m
        ps[k, 0:row] = g.astype(BF16)
        ps[k, row : 2 * row] = m.astype(BF16)
        return carry

    lax.fori_loop(0, NZ, pack, 0)
    store_m = pltpu.make_async_copy(mv, mom_o, out_sem.at[0])
    store_m.start()
    pr[z] = ps[z]

    for way in range(2):
        left_z(0, way).wait_recv()
        left_z(1, way).start()
    for d in FILL:
        packed_z(d)
    left_send(near(1))
    left_pass(own)

    wait(right.at[pl.ds(0, 4)], rz_r.at[0])
    for zz in near(1) + near(2):
        right_x(zz)
    wait(right.at[pl.ds(0, 3)], rz_r.at[1])
    for zz in near(3) + [up(z, 4, NZ)]:
        right_x(zz)

    for way in range(2):
        left_z(1, way).wait_recv()
        left_z(2, way).start()
        left_z(3, way).start()
    for d in REST:
        packed_z(d)
    left_send(two)
    left_pass(near(1))
    left_share(own)

    right_core(x, 0).start()
    for way in range(2):
        wait(rb.at[:, x, c], rx_r.at[way])
        right_half(way).start()
        right_core(up(x, -1 if way == 0 else 1, NX), 1 + way).start()

    for way in range(2):
        left_z(2, way).wait_recv()
        left_z(3, way).wait_recv()
    left_send(last)
    left_pass(two)
    left_share(near(1))

    for way in range(2):
        right_half(way).wait_recv()
    right_core(up(x, 2, NX), 3).start()
    for i in range(4):
        right_core(x, i).wait_recv()

    def order(i):
        d = z
        for step, other_d in enumerate(FILL + REST):
            d = jnp.where(i == step + 1, up(z, -other_d, NZ), d)
        return d

    def turn(i, carry):
        zz = order(i)

        @pl.when(i > 0)
        def _():
            wait(pr.at[zz], pz_r.at[zz])

        t = jnp.dot(pr[zz], rb[...].reshape(width, width), preferred_element_type=F32).astype(BF16)
        seg = width // NP
        for q in range(NP):
            tb[zz, q, :, 0:seg] = t[0:row, q * seg : (q + 1) * seg]
            tb[zz, q, :, seg : 2 * seg] = t[row : 2 * row, q * seg : (q + 1) * seg]
        cb[zz, p] = tb[zz, p]

        def send(e, carry):
            q = lax.rem(p + e, NP)
            remote(tb.at[zz, q], cb.at[zz, p], tx_s, tx_r.at[zz], {"fsdp": z * NP + q}).start()
            return carry

        lax.fori_loop(1, NP, send, 0)
        return carry

    lax.fori_loop(0, 3, turn, 0)
    left_pass(last)
    left_share(two)
    lax.fori_loop(3, 5, turn, 0)
    left_share(last)
    lax.fori_loop(5, 8, turn, 0)

    def left_done(zz, carry):
        left_core(zz).wait_recv()
        return carry

    lax.fori_loop(0, NZ, left_done, 0)
    seg = width // NP
    part = width // 4

    def project(i, carry):
        zz = order(i)
        l, q = zz // 4, lax.rem(zz, 4)
        wait(cb.at[zz, pl.ds(0, NP - 1)], tx_r.at[zz])
        turned = cb[zz].reshape(NP * row, 2 * seg)
        for k in range(4):
            at = slice(k * part, (k + 1) * part)
            basis = lb[l, pl.ds(2 * q, 2), :, :, :, at].reshape(NP * row, part)
            ac[l, at] += lax.dot_general(basis, turned, (((0,), (0,)), ((), ())), preferred_element_type=F32)
        return carry

    lax.fori_loop(0, NZ, project, 0)
    loads[4].wait()

    def scale(l):
        def piece(i, carry):
            inside = pl.ds(pl.multiple_of(i * part, part), part)
            rows = pl.ds(pl.multiple_of(l * width + i * part, part), part)
            g, m = ac[l, inside, :seg], ac[l, inside, seg:]
            s = BETA_TWO * sv[rows, :] + (1.0 - BETA_TWO) * g * g
            sv[rows, :] = s
            sc[rows, :] = (m / (jnp.sqrt(s) + EPSILON)).astype(BF16)
            return carry

        lax.fori_loop(0, 4, piece, 0)

    def far(i):
        d = (NZ - i) // 2
        return up(z, jnp.where(lax.rem(i, 2) == 1, d, -d), NZ)

    def back(i, carry):
        zz = far(i)
        l, q = zz // 4, lax.rem(zz, 4)
        basis = lb[l, pl.ds(2 * q, 2)].reshape(NP * row, width)
        scaled = sc[pl.ds(pl.multiple_of(l * width, width), width), :]
        out = jnp.dot(basis, scaled, preferred_element_type=F32).astype(BF16)
        bk[zz] = out.reshape(NP, row, seg)
        wb[zz, p] = bk[zz, p]

        def send(e, carry):
            q = lax.rem(p + e, NP)
            remote(bk.at[zz, q], wb.at[zz, p], bx_s, bx_r.at[zz], {"fsdp": z * NP + q}).start()
            return carry

        lax.fori_loop(1, NP, send, 0)
        return carry

    first = up(z, 4, NZ) // 4
    scale(first)
    lax.fori_loop(0, 1, back, 0)
    scale(1 - first)
    store_s = pltpu.make_async_copy(sv, sec_o, out_sem.at[1])
    store_s.start()
    lax.fori_loop(1, NZ, back, 0)

    mine = pl.ds(pl.multiple_of(z * width, width), width)

    def update(i, carry):
        zz = far(i)
        wait(wb.at[zz, pl.ds(0, NP - 1)], bx_r.at[zz])
        rows = jnp.concatenate([wb[zz, q] for q in range(NP)], axis=1)
        out = lax.dot_general(
            rows, rb[...].reshape(width, width), (((1,), (1,)), ((), ())), preferred_element_type=F32
        )
        ub[zz] = out.astype(BF16)

        @pl.when(i < NZ - 1)
        def _():
            remote(ub.at[zz], upd_o.at[:, mine], uz_s, uz_r, dev(zz, x, c)).start()

        return carry

    lax.fori_loop(0, NZ, update, 0)
    store_u = pltpu.make_async_copy(ub.at[z], upd_o.at[:, mine], out_sem.at[2])
    store_u.start()

    for way in range(2):
        wait(rb.at[:, x, c], rx_s.at[way])
        right_half(way).wait_send()
        for step in range(4):
            left_z(step, way).wait_send()
    for i in range(4):
        right_core(x, i).wait_send()

    def drain(zz, carry):
        for way in range(2):
            left_x(zz, way).wait_send()
            left_half(zz, way).wait_send()
        left_core(zz).wait_send()
        return carry

    lax.fori_loop(0, NZ, drain, 0)
    wait(right.at[pl.ds(0, NZ - 1)], rz_s)
    wait(ps.at[pl.ds(0, NZ - 1)], pz_s)
    wait(tb.at[pl.ds(0, NZ - 1)], tx_s)
    wait(bk.at[pl.ds(0, NZ - 1)], bx_s)
    wait(ub.at[pl.ds(0, NZ - 1)], uz_s)
    wait(ub.at[pl.ds(0, NZ - 1)], uz_r)
    store_m.wait()
    store_s.wait()
    store_u.wait()


def finish(update, mom, sec, upd_o, mom_o, sec_o, ub, uf, mb, sb, sem):
    parts = 4
    step = uf.shape[1] // parts
    cols = [pl.ds(i * step, step) for i in range(parts)]
    loads = [pltpu.make_async_copy(update.at[:, at], ub.at[:, at], sem.at[i]) for i, at in enumerate(cols)]
    loads += [pltpu.make_async_copy(mom, mb, sem.at[parts]), pltpu.make_async_copy(sec, sb, sem.at[parts + 1])]
    for load in loads:
        load.start()
    stores = []
    for i, at in enumerate(cols):
        loads[i].wait()
        uf[:, at] = ub[:, at].astype(F32)
        stores.append(pltpu.make_async_copy(uf.at[:, at], upd_o.at[:, at], sem.at[parts + 2 + i]))
        stores[-1].start()
    for i, (held, out) in enumerate(((mb, mom_o), (sb, sec_o))):
        loads[parts + i].wait()
        stores.append(pltpu.make_async_copy(held, out, sem.at[2 * parts + 2 + i]))
        stores[-1].start()
    for store in stores:
        store.wait()


def local(grad, moment, second, left_basis, right_basis):
    row, cols = grad.shape
    lblocks, piece, width = left_basis.shape
    total, seg = second.shape
    any_spec = pl.BlockSpec(memory_space=pl.ANY)
    dma = pltpu.SemaphoreType.DMA
    update, moment_new, second_new = pl.pallas_call(
        kernel,
        out_shape=(
            jax.ShapeDtypeStruct((row, cols), BF16),
            jax.ShapeDtypeStruct((row, cols), F32),
            jax.ShapeDtypeStruct((total, seg), F32),
        ),
        in_specs=[any_spec] * 5,
        out_specs=[any_spec] * 3,
        scratch_shapes=[
            pltpu.VMEM((row, cols), F32),
            pltpu.VMEM((row, cols), F32),
            pltpu.VMEM((total, seg), F32),
            pltpu.VMEM((NZ, 2 * row, width), BF16),
            pltpu.VMEM((NZ, 2 * row, width), BF16),
            pltpu.VMEM((NZ, NX, NC, piece, width), BF16),
            pltpu.VMEM((NZ, NP, row, 2 * seg), BF16),
            pltpu.VMEM((NZ, NP, row, 2 * seg), BF16),
            pltpu.VMEM((lblocks, NZ, NX, NC, piece, width), BF16),
            pltpu.VMEM((lblocks, width, 2 * seg), F32),
            pltpu.VMEM((total, seg), BF16),
            pltpu.VMEM((NZ, NP, row, seg), BF16),
            pltpu.VMEM((NZ, NP, row, seg), BF16),
            pltpu.VMEM((NZ, row, width), BF16),
            dma((5,)), dma((3,)),
            dma, dma((2,)), dma((4,)), dma((4,)), dma((4,)), dma((4,)),
            dma((4, 2)), dma((4, 2)), dma((NZ, 2)), dma((NZ, 2)), dma((NZ, 2)), dma((NZ, 2)), dma((NZ,)), dma((NZ,)),
            dma, dma((NZ,)), dma, dma((NZ,)), dma, dma((NZ,)), dma, dma,
        ],
        compiler_params=pltpu.CompilerParams(
            collective_id=0, has_side_effects=True, vmem_limit_bytes=62 * 2**20
        ),
        cost_estimate=pl.CostEstimate(flops=3 * 2**30, bytes_accessed=8 * 2**20, transcendentals=2**19),
        name="soap_step",
    )(grad, moment, second, left_basis, right_basis)
    return pl.pallas_call(
        finish,
        out_shape=(
            jax.ShapeDtypeStruct((row, cols), F32),
            jax.ShapeDtypeStruct((row, cols), F32),
            jax.ShapeDtypeStruct((total, seg), F32),
        ),
        in_specs=[any_spec] * 3,
        out_specs=[pl.BlockSpec(memory_space=pltpu.MemorySpace.HBM)] * 3,
        scratch_shapes=[pltpu.VMEM((row, cols), BF16), pltpu.VMEM((row, cols), F32), pltpu.VMEM((row, cols), F32), pltpu.VMEM((total, seg), F32), dma((12,))],
        compiler_params=pltpu.CompilerParams(vmem_limit_bytes=62 * 2**20),
        name="finish",
    )(update, moment_new, second_new)


def solution(mesh):
    in_specs = (
        P(("dp", "fsdp"), None),
        P(("dp", "fsdp"), None),
        P("dp", "fsdp"),
        P("dp", "fsdp", None),
        P("dp", "fsdp", None),
    )
    out_specs = (P(("dp", "fsdp"), None), P(("dp", "fsdp"), None), P("dp", "fsdp"))
    return jax.shard_map(local, mesh=mesh, in_specs=in_specs, out_specs=out_specs, check_vma=False)
```

```python
import jax
import jax.numpy as jnp
from jax import lax
from jax.experimental import pallas as pl
from jax.experimental.pallas import tpu as pltpu
from jax.sharding import PartitionSpec as P

BETA_ONE = 0.9
BETA_TWO = 0.95
EPSILON = 1e-08

NZ, NX, NC = 8, 4, 2
NP = NX * NC
F32, BF16 = jnp.float32, jnp.bfloat16

FILL = (1, -1)
REST = (2, -2, 3, -3, 4)
LAST = REST[-1]

RETURN = (3, -3, 2, -2, 4, 1, -1)


def kernel(
    grad, moment, second, left, right,
    upd_o, mom_o, sec_o,
    gv, mv, sv, ps, pr, rb, tb, cb, lb, ac, sc, bk, wb, ub,
    in_sem, out_sem,
    rz_s, rz_r, rx_s, rx_r, rd_s, rd_r,
    lz_s, lz_r, lx_s, lx_r, lo_s, lo_r, ld_s, ld_r,
    pz_s, pz_r, pl_r, tx_s, tx_r, bx_s, bx_r, uz_s, uz_r,
):
    f = lax.axis_index("fsdp")
    z, p = f // NP, lax.rem(f, NP)
    x, c = p // NC, lax.rem(p, NC)
    row = gv.shape[0]
    width = rb.shape[-1]

    def dev(zz, xx, cc):
        return {"fsdp": (zz * NX + xx) * NC + cc}

    def up(v, d, n):
        return lax.rem(v + d + 2 * n, n)

    def zdev(d):
        return dev(up(z, d, NZ), x, c)

    def xdev(d):
        return dev(z, up(x, d, NX), c)

    other = dev(z, x, 1 - c)

    def remote(src, dst, ss, rs, to):
        return pltpu.make_async_remote_copy(
            src_ref=src, dst_ref=dst, send_sem=ss, recv_sem=rs, device_id=to, device_id_type=pl.DeviceIdType.MESH
        )

    def wait(ref, sem):
        pltpu.make_async_copy(ref, ref, sem).wait()

    barrier = pltpu.get_barrier_semaphore()
    for d in (4, 3, -3, 2, -2, 1, -1):
        pl.semaphore_signal(barrier, inc=1, device_id=zdev(d), device_id_type=pl.DeviceIdType.MESH)
    for d in range(1, NP):
        to = {"fsdp": z * NP + lax.rem(p + d, NP)}
        pl.semaphore_signal(barrier, inc=1, device_id=to, device_id_type=pl.DeviceIdType.MESH)

    loads = [
        pltpu.make_async_copy(left, lb.at[:, z, x, c], in_sem.at[0]),
        pltpu.make_async_copy(right.at[z], rb.at[z, x, c], in_sem.at[1]),
        pltpu.make_async_copy(grad, gv, in_sem.at[2]),
        pltpu.make_async_copy(moment, mv, in_sem.at[3]),
        pltpu.make_async_copy(second, sv, in_sem.at[4]),
    ]
    for load in loads:
        load.start()
    ac[...] = jnp.zeros_like(ac)
    loads[0].wait()
    loads[1].wait()
    pl.semaphore_wait(barrier, 2 * (NZ - 1))

    def right_z(d):
        group = 0 if abs(d) <= 2 else 1
        remote(right.at[up(z, d, NZ)], rb.at[z, x, c], rz_s, rz_r.at[group], zdev(d)).start()

    def left_z(step, way):
        sign = 1 if way == 0 else -1
        blk = up(z, -(0, 1, 2, 2)[step] * sign, NZ)
        ref = lb.at[way, blk, x, c] if step == 3 else lb.at[:, blk, x, c]
        return remote(ref, ref, lz_s.at[step, way], lz_r.at[step, way], zdev((1, 1, 1, 2)[step] * sign))

    def packed_z(d):
        k = up(z, d, NZ)
        if d != LAST:
            remote(ps.at[k], pr.at[z], pz_s, pz_r.at[z], dev(k, x, c)).start()
            return
        for h in range(2):
            rows = pl.ds(h * (row // 2), row // 2)
            remote(ps.at[k, :, rows], pr.at[z, :, rows], pz_s, pl_r.at[h], dev(k, x, c)).start()

    def right_x(zz):
        ref = rb.at[zz, x, c]
        for way in range(2):
            remote(ref, ref, rx_s.at[way], rx_r.at[way], xdev(1 if way == 0 else -1)).start()

    def right_half(way):
        ref = rb.at[pl.ds(way * (NZ // 2), NZ // 2), up(x, -1 if way == 0 else 1, NX), c]
        return remote(ref, ref, rx_s.at[2 + way], rx_r.at[2 + way], xdev(1 if way == 0 else -1))

    def right_core(xx, i):
        ref = rb.at[:, xx, c]
        return remote(ref, ref, rd_s.at[i], rd_r.at[i], other)

    def left_x(zz, way):
        ref = lb.at[:, zz, x, c]
        return remote(ref, ref, lx_s.at[zz, way], lx_r.at[zz, way], xdev(1 if way == 0 else -1))

    def left_half(zz, way):
        ref = lb.at[way, zz, up(x, -1 if way == 0 else 1, NX), c]
        return remote(ref, ref, lo_s.at[zz, way], lo_r.at[zz, way], xdev(1 if way == 0 else -1))

    def left_core(zz):
        ref = lb.at[:, zz, :, c]
        return remote(ref, ref, ld_s.at[zz], ld_r.at[zz], other)

    def near(d):
        return [up(z, -d, NZ), up(z, d, NZ)]

    def left_opposite(way):
        ref = lb.at[way, z, x, c]
        return remote(ref, ref, lo_s.at[z, way], lo_r.at[z, way], xdev(2))

    def left_send(group):
        for zz in group:
            for way in range(2):
                left_x(zz, way).start()

    def left_pass(group):
        for zz in group:
            for way in range(2):
                left_x(zz, way).wait_recv()
                left_half(zz, way).start()

    def left_share(group):
        for zz in group:
            for way in range(2):
                left_half(zz, way).wait_recv()
            left_core(zz).start()

    own, two, last = [z], near(2), near(3) + [up(z, 4, NZ)]

    for way in range(2):
        left_z(0, way).start()
    left_send(own)
    right_x(z)
    for way in range(2):
        left_opposite(way).start()
    for d in (1, -1, 2, -2, 3, -3, 4):
        right_z(d)

    loads[2].wait()
    loads[3].wait()

    def pack(k, carry):
        cols = pl.ds(pl.multiple_of(k * width, width), width)
        g = gv[:, cols]
        m = BETA_ONE * mv[:, cols] + (1.0 - BETA_ONE) * g
        mv[:, cols] = m
        ps[k, 0] = g.astype(BF16)
        ps[k, 1] = m.astype(BF16)
        return carry

    lax.fori_loop(0, NZ, pack, 0)
    store_m = pltpu.make_async_copy(mv, mom_o, out_sem.at[0])
    store_m.start()
    pr[z] = ps[z]

    for way in range(2):
        left_z(0, way).wait_recv()
        left_z(1, way).start()
    for d in FILL:
        packed_z(d)
    left_send(near(1))

    wait(right.at[pl.ds(0, 4)], rz_r.at[0])
    for zz in near(1) + near(2):
        right_x(zz)
    left_pass(near(1))
    wait(right.at[pl.ds(0, 3)], rz_r.at[1])
    for zz in near(3) + [up(z, 4, NZ)]:
        right_x(zz)

    for way in range(2):
        left_z(1, way).wait_recv()
        left_z(2, way).start()
        left_z(3, way).start()
    for d in REST:
        packed_z(d)
    left_send(two)
    for way in range(2):
        left_x(z, way).wait_recv()
    left_share(own)

    right_core(x, 0).start()
    for way in range(2):
        wait(rb.at[:, x, c], rx_r.at[way])
        right_half(way).start()
        right_core(up(x, -1 if way == 0 else 1, NX), 1 + way).start()

    for way in range(2):
        left_z(2, way).wait_recv()
    left_send(near(3))
    left_pass(two)
    left_share(near(1))
    for way in range(2):
        left_z(3, way).wait_recv()
    left_send([up(z, 4, NZ)])

    for way in range(2):
        right_half(way).wait_recv()
    right_core(up(x, 2, NX), 3).start()
    for i in range(4):
        right_core(x, i).wait_recv()

    def order(i):
        d = z
        for step, other_d in enumerate(FILL + REST):
            d = jnp.where(i == step + 1, up(z, -other_d, NZ), d)
        return d

    def turn_rows(zz, h0, rows):
        at = pl.ds(h0, rows)
        both = pr[zz, :, at].reshape(2 * rows, width)
        t = jnp.dot(both, rb[...].reshape(width, width), preferred_element_type=F32).astype(BF16)
        seg = width // NP
        for q in range(NP):
            tb[zz, q, at, 0:seg] = t[0:rows, q * seg : (q + 1) * seg]
            tb[zz, q, at, seg : 2 * seg] = t[rows : 2 * rows, q * seg : (q + 1) * seg]
        cb[zz, p, at] = tb[zz, p, at]

        def send(e, carry):
            q = lax.rem(p + e, NP)
            remote(tb.at[zz, q, at], cb.at[zz, p, at], tx_s, tx_r.at[zz], {"fsdp": z * NP + q}).start()
            return carry

        lax.fori_loop(1, NP, send, 0)

    def turn(i, carry):
        zz = order(i)

        @pl.when(i > 0)
        def _():
            wait(pr.at[zz], pz_r.at[zz])

        turn_rows(zz, 0, row)
        return carry

    def turn_last(h, carry):
        half = row // 2
        wait(pr.at[0, :, pl.ds(0, half)], pl_r.at[h])
        turn_rows(up(z, -LAST, NZ), pl.multiple_of(h * half, half), half)
        return carry

    lax.fori_loop(0, 3, turn, 0)
    left_pass(last)
    left_share(two)
    lax.fori_loop(3, 5, turn, 0)
    left_share(last)
    lax.fori_loop(5, 7, turn, 0)
    lax.fori_loop(0, 2, turn_last, 0)

    def left_done(zz, carry):
        left_core(zz).wait_recv()
        return carry

    lax.fori_loop(0, NZ, left_done, 0)
    seg = width // NP
    part = width // 4

    def project(i, carry):
        zz = order(i)
        l, q = zz // 4, lax.rem(zz, 4)
        wait(cb.at[zz, pl.ds(0, NP - 1)], tx_r.at[zz])
        turned = cb[zz].reshape(NP * row, 2 * seg)
        for k in range(4):
            at = slice(k * part, (k + 1) * part)
            basis = lb[l, pl.ds(2 * q, 2), :, :, :, at].reshape(NP * row, part)
            ac[l, at] += lax.dot_general(basis, turned, (((0,), (0,)), ((), ())), preferred_element_type=F32)
        return carry

    lax.fori_loop(0, NZ, project, 0)
    loads[4].wait()

    def scale(l):
        def piece(i, carry):
            inside = pl.ds(pl.multiple_of(i * part, part), part)
            rows = pl.ds(pl.multiple_of(l * width + i * part, part), part)
            g, m = ac[l, inside, :seg], ac[l, inside, seg:]
            s = BETA_TWO * sv[rows, :] + (1.0 - BETA_TWO) * g * g
            sv[rows, :] = s
            sc[rows, :] = (m / (jnp.sqrt(s) + EPSILON)).astype(BF16)
            return carry

        lax.fori_loop(0, 4, piece, 0)

    def far(i):
        zz = z
        for step, d in enumerate(RETURN):
            zz = jnp.where(i == step, up(z, d, NZ), zz)
        return zz

    def back(i, carry):
        zz = far(i)
        l, q = zz // 4, lax.rem(zz, 4)
        basis = lb[l, pl.ds(2 * q, 2)].reshape(NP * row, width)
        scaled = sc[pl.ds(pl.multiple_of(l * width, width), width), :]
        out = jnp.dot(basis, scaled, preferred_element_type=F32).astype(BF16)
        bk[zz] = out.reshape(NP, row, seg)
        wb[zz, p] = bk[zz, p]

        def send(e, carry):
            q = lax.rem(p + e, NP)
            remote(bk.at[zz, q], wb.at[zz, p], bx_s, bx_r.at[zz], {"fsdp": z * NP + q}).start()
            return carry

        lax.fori_loop(1, NP, send, 0)
        return carry

    first = up(z, RETURN[0], NZ) // 4
    scale(first)
    lax.fori_loop(0, 1, back, 0)
    scale(1 - first)
    store_s = pltpu.make_async_copy(sv, sec_o, out_sem.at[1])
    store_s.start()
    lax.fori_loop(1, NZ, back, 0)

    mine = pl.ds(pl.multiple_of(z * width, width), width)

    def update(i, carry):
        zz = far(i)
        wait(wb.at[zz, pl.ds(0, NP - 1)], bx_r.at[zz])
        rows = jnp.concatenate([wb[zz, q] for q in range(NP)], axis=1)
        out = lax.dot_general(
            rows, rb[...].reshape(width, width), (((1,), (1,)), ((), ())), preferred_element_type=F32
        )
        ub[zz] = out.astype(BF16)

        @pl.when(i < NZ - 1)
        def _():
            remote(ub.at[zz], upd_o.at[:, mine], uz_s, uz_r, dev(zz, x, c)).start()

        return carry

    lax.fori_loop(0, NZ, update, 0)
    store_u = pltpu.make_async_copy(ub.at[z], upd_o.at[:, mine], out_sem.at[2])
    store_u.start()

    for way in range(2):
        wait(rb.at[:, x, c], rx_s.at[way])
        right_half(way).wait_send()
        for step in range(4):
            left_z(step, way).wait_send()
    for i in range(4):
        right_core(x, i).wait_send()

    def drain(zz, carry):
        for way in range(2):
            left_x(zz, way).wait_send()
            left_half(zz, way).wait_send()
        left_core(zz).wait_send()
        return carry

    lax.fori_loop(0, NZ, drain, 0)
    wait(right.at[pl.ds(0, NZ - 1)], rz_s)
    wait(ps.at[pl.ds(0, NZ - 1)], pz_s)
    wait(tb.at[pl.ds(0, NZ - 1)], tx_s)
    wait(bk.at[pl.ds(0, NZ - 1)], bx_s)
    wait(ub.at[pl.ds(0, NZ - 1)], uz_s)
    wait(ub.at[pl.ds(0, NZ - 1)], uz_r)
    store_m.wait()
    store_s.wait()
    store_u.wait()


def finish(update, mom, sec, upd_o, mom_o, sec_o, ub, uf, sem):
    parts = 4
    step = uf.shape[1] // parts
    cols = [pl.ds(i * step, step) for i in range(parts)]
    loads = [pltpu.make_async_copy(update.at[:, at], ub.at[:, at], sem.at[i]) for i, at in enumerate(cols)]
    stores = [pltpu.make_async_copy(mom, mom_o, sem.at[parts]), pltpu.make_async_copy(sec, sec_o, sem.at[parts + 1])]
    for copy in loads + stores:
        copy.start()
    for i, at in enumerate(cols):
        loads[i].wait()
        uf[:, at] = ub[:, at].astype(F32)
        stores.append(pltpu.make_async_copy(uf.at[:, at], upd_o.at[:, at], sem.at[parts + 2 + i]))
        stores[-1].start()
    for store in stores:
        store.wait()


def local(grad, moment, second, left_basis, right_basis):
    row, cols = grad.shape
    lblocks, piece, width = left_basis.shape
    total, seg = second.shape
    any_spec = pl.BlockSpec(memory_space=pl.ANY)
    dma = pltpu.SemaphoreType.DMA
    update, moment_new, second_new = pl.pallas_call(
        kernel,
        out_shape=(pltpu.VMEM((row, cols), BF16), pltpu.VMEM((row, cols), F32), pltpu.VMEM((total, seg), F32)),
        in_specs=[any_spec] * 5,
        out_specs=[any_spec] * 3,
        scratch_shapes=[
            pltpu.VMEM((row, cols), F32),
            pltpu.VMEM((row, cols), F32),
            pltpu.VMEM((total, seg), F32),
            pltpu.VMEM((NZ, 2, row, width), BF16),
            pltpu.VMEM((NZ, 2, row, width), BF16),
            pltpu.VMEM((NZ, NX, NC, piece, width), BF16),
            pltpu.VMEM((NZ, NP, row, 2 * seg), BF16),
            pltpu.VMEM((NZ, NP, row, 2 * seg), BF16),
            pltpu.VMEM((lblocks, NZ, NX, NC, piece, width), BF16),
            pltpu.VMEM((lblocks, width, 2 * seg), F32),
            pltpu.VMEM((total, seg), BF16),
            pltpu.VMEM((NZ, NP, row, seg), BF16),
            pltpu.VMEM((NZ, NP, row, seg), BF16),
            pltpu.VMEM((NZ, row, width), BF16),
            dma((5,)), dma((3,)),
            dma, dma((2,)), dma((4,)), dma((4,)), dma((4,)), dma((4,)),
            dma((4, 2)), dma((4, 2)), dma((NZ, 2)), dma((NZ, 2)), dma((NZ, 2)), dma((NZ, 2)), dma((NZ,)), dma((NZ,)),
            dma, dma((NZ,)), dma((2,)), dma, dma((NZ,)), dma, dma((NZ,)), dma, dma,
        ],
        compiler_params=pltpu.CompilerParams(
            collective_id=0, has_side_effects=True, vmem_limit_bytes=61 * 2**20 + 2**18
        ),
        cost_estimate=pl.CostEstimate(flops=3 * 2**30, bytes_accessed=8 * 2**20, transcendentals=2**19),
        name="soap_step",
    )(grad, moment, second, left_basis, right_basis)
    return pl.pallas_call(
        finish,
        out_shape=(
            jax.ShapeDtypeStruct((row, cols), F32),
            jax.ShapeDtypeStruct((row, cols), F32),
            jax.ShapeDtypeStruct((total, seg), F32),
        ),
        in_specs=[any_spec] * 3,
        out_specs=[pl.BlockSpec(memory_space=pltpu.MemorySpace.HBM)] * 3,
        scratch_shapes=[pltpu.VMEM((row, cols), BF16), pltpu.VMEM((row, cols), F32), dma((10,))],
        compiler_params=pltpu.CompilerParams(vmem_limit_bytes=16 * 2**20),
        name="finish",
    )(update, moment_new, second_new)


def solution(mesh):
    in_specs = (
        P(("dp", "fsdp"), None),
        P(("dp", "fsdp"), None),
        P("dp", "fsdp"),
        P("dp", "fsdp", None),
        P("dp", "fsdp", None),
    )
    out_specs = (P(("dp", "fsdp"), None), P(("dp", "fsdp"), None), P("dp", "fsdp"))
    return jax.shard_map(local, mesh=mesh, in_specs=in_specs, out_specs=out_specs, check_vma=False)
```

```python
import jax
import jax.numpy as jnp
from jax import lax
from jax.experimental import pallas as pl
from jax.experimental.pallas import tpu as pltpu
from jax.sharding import PartitionSpec as P

BETA_ONE = 0.9
BETA_TWO = 0.95
EPSILON = 1e-08

NZ, NX, NC = 8, 4, 2
NP = NX * NC
F32, BF16 = jnp.float32, jnp.bfloat16

FILL = (1, -1)
REST = (2, -2, 3, -3, 4)
LAST = REST[-1]

RETURN = (3, -3, 2, -2, 4, 1, -1)


def kernel(
    grad, moment, second, left, right,
    upd_o, mom_o, sec_o,
    gv, mv, sv, ps, pr, rb, rt, tb, cb, lb, ac, sc, bk, wb, ub,
    here, in_sem, out_sem,
    rz_s, rz_r, rx_s, rx_r, rd_s, rd_r,
    lz_s, lz_r, lx_s, lx_r, lo_s, lo_r, ld_s, ld_r,
    pz_s, pz_r, pl_r, tx_s, tx_r, bx_s, bx_r, uz_s, uz_r,
):
    f = lax.axis_index("fsdp")
    z, p = f // NP, lax.rem(f, NP)
    x, c = p // NC, lax.rem(p, NC)
    row = gv.shape[0]
    width = rb.shape[-1]

    def dev(zz, xx, cc):
        return {"fsdp": (zz * NX + xx) * NC + cc}

    def up(v, d, n):
        return lax.rem(v + d + 2 * n, n)

    def zdev(d):
        return dev(up(z, d, NZ), x, c)

    def xdev(d):
        return dev(z, up(x, d, NX), c)

    other = dev(z, x, 1 - c)

    def remote(src, dst, ss, rs, to):
        return pltpu.make_async_remote_copy(
            src_ref=src, dst_ref=dst, send_sem=ss, recv_sem=rs, device_id=to, device_id_type=pl.DeviceIdType.MESH
        )

    def wait(ref, sem):
        pltpu.make_async_copy(ref, ref, sem).wait()

    barrier = pltpu.get_barrier_semaphore()
    for d in (1, -1):
        pl.semaphore_signal(barrier, inc=1, device_id=zdev(d), device_id_type=pl.DeviceIdType.MESH)
    for d in range(1, NP):
        to = {"fsdp": z * NP + lax.rem(p + d, NP)}
        pl.semaphore_signal(barrier, inc=1, device_id=to, device_id_type=pl.DeviceIdType.MESH)

    loads = [
        pltpu.make_async_copy(left, lb.at[:, z, x, c], in_sem.at[0]),
        pltpu.make_async_copy(right.at[z], rb.at[z, x, c], in_sem.at[1]),
        pltpu.make_async_copy(grad, gv, in_sem.at[2]),
        pltpu.make_async_copy(moment, mv, in_sem.at[3]),
        pltpu.make_async_copy(second, sv, in_sem.at[4]),
    ]
    for load in loads:
        load.start()
    ac[...] = jnp.zeros_like(ac)
    loads[0].wait()
    loads[1].wait()
    pl.semaphore_wait(barrier, 2 + NP - 1)

    def right_z(d):
        group = 0 if abs(d) <= 2 else 1
        remote(right.at[up(z, d, NZ)], rb.at[z, x, c], rz_s, rz_r.at[group], zdev(d)).start()

    def left_z(step, way):
        sign = 1 if way == 0 else -1
        blk = up(z, -(0, 1, 2, 2)[step] * sign, NZ)
        ref = lb.at[way, blk, x, c] if step == 3 else lb.at[:, blk, x, c]
        return remote(ref, ref, lz_s.at[step, way], lz_r.at[step, way], zdev((1, 1, 1, 2)[step] * sign))

    def packed_z(d):
        k = up(z, d, NZ)
        if d != LAST:
            remote(ps.at[k], pr.at[z], pz_s, pz_r.at[z], dev(k, x, c)).start()
            return
        for h in range(2):
            rows = pl.ds(h * (row // 2), row // 2)
            remote(ps.at[k, :, rows], pr.at[z, :, rows], pz_s, pl_r.at[h], dev(k, x, c)).start()

    def right_x(zz):
        ref = rb.at[zz, x, c]
        for way in range(2):
            remote(ref, ref, rx_s.at[way], rx_r.at[way], xdev(1 if way == 0 else -1)).start()

    def right_half(way):
        ref = rb.at[pl.ds(way * (NZ // 2), NZ // 2), up(x, -1 if way == 0 else 1, NX), c]
        return remote(ref, ref, rx_s.at[2 + way], rx_r.at[2 + way], xdev(1 if way == 0 else -1))

    def right_core(xx, i):
        ref = rb.at[:, xx, c]
        return remote(ref, ref, rd_s.at[i], rd_r.at[i], other)

    def left_x(zz, way):
        ref = lb.at[:, zz, x, c]
        return remote(ref, ref, lx_s.at[zz, way], lx_r.at[zz, way], xdev(1 if way == 0 else -1))

    def left_half(zz, way):
        ref = lb.at[way, zz, up(x, -1 if way == 0 else 1, NX), c]
        return remote(ref, ref, lo_s.at[zz, way], lo_r.at[zz, way], xdev(1 if way == 0 else -1))

    def left_core(zz):
        ref = lb.at[:, zz, :, c]
        return remote(ref, ref, ld_s.at[zz], ld_r.at[zz], other)

    def near(d):
        return [up(z, -d, NZ), up(z, d, NZ)]

    def left_opposite(way):
        ref = lb.at[way, z, x, c]
        return remote(ref, ref, lo_s.at[z, way], lo_r.at[z, way], xdev(2))

    def left_send(group):
        for zz in group:
            for way in range(2):
                left_x(zz, way).start()

    def left_pass(group):
        for zz in group:
            for way in range(2):
                left_x(zz, way).wait_recv()
                left_half(zz, way).start()

    def left_share(group):
        for zz in group:
            for way in range(2):
                left_half(zz, way).wait_recv()
            left_core(zz).start()

    own, two, last = [z], near(2), near(3) + [up(z, 4, NZ)]

    for way in range(2):
        left_z(0, way).start()
    left_send(own)
    right_x(z)
    for way in range(2):
        left_opposite(way).start()
    for d in (1, -1):
        right_z(d)

    for s in range(1, NZ // 2):
        ways = range(2) if s < NZ // 2 - 1 else range(1)
        for way in ways:
            to = zdev(1 if way == 0 else -1)
            pl.semaphore_signal(here.at[s - 1, way], inc=1, device_id=to, device_id_type=pl.DeviceIdType.MESH)
        for way in ways:
            pl.semaphore_wait(here.at[s - 1, way], 1)
        for way in ways:
            right_z(s + 1 if way == 0 else -s - 1)

    loads[2].wait()
    loads[3].wait()

    def pack(k, carry):
        cols = pl.ds(pl.multiple_of(k * width, width), width)
        g = gv[:, cols]
        m = BETA_ONE * mv[:, cols] + (1.0 - BETA_ONE) * g
        mv[:, cols] = m
        ps[k, 0] = g.astype(BF16)
        ps[k, 1] = m.astype(BF16)
        return carry

    lax.fori_loop(0, NZ, pack, 0)
    store_m = pltpu.make_async_copy(mv, mom_o, out_sem.at[0])
    store_m.start()
    pr[z] = ps[z]

    for way in range(2):
        left_z(0, way).wait_recv()
        left_z(1, way).start()
    for d in FILL:
        packed_z(d)
    left_send(near(1))

    wait(right.at[pl.ds(0, 4)], rz_r.at[0])
    for zz in near(1) + near(2):
        right_x(zz)
    left_pass(near(1))
    wait(right.at[pl.ds(0, 3)], rz_r.at[1])
    for zz in near(3) + [up(z, 4, NZ)]:
        right_x(zz)

    for way in range(2):
        left_z(1, way).wait_recv()
        left_z(2, way).start()
        left_z(3, way).start()
    for d in REST:
        packed_z(d)
    left_send(two)
    for way in range(2):
        left_x(z, way).wait_recv()
    left_share(own)

    right_core(x, 0).start()
    for way in range(2):
        wait(rb.at[:, x, c], rx_r.at[way])
        right_half(way).start()
        right_core(up(x, -1 if way == 0 else 1, NX), 1 + way).start()

    for way in range(2):
        left_z(2, way).wait_recv()
    left_send(near(3))
    left_pass(two)
    left_share(near(1))
    for way in range(2):
        left_z(3, way).wait_recv()
    left_send([up(z, 4, NZ)])

    for way in range(2):
        right_half(way).wait_recv()
    right_core(up(x, 2, NX), 3).start()
    for i in range(4):
        right_core(x, i).wait_recv()

    def order(i):
        d = z
        for step, other_d in enumerate(FILL + REST):
            d = jnp.where(i == step + 1, up(z, -other_d, NZ), d)
        return d

    def turn_rows(zz, h0, rows):
        at = pl.ds(h0, rows)
        both = pr[zz, :, at].reshape(2 * rows, width)
        t = jnp.dot(both, rb[...].reshape(width, width), preferred_element_type=F32).astype(BF16)
        seg = width // NP
        for q in range(NP):
            tb[zz, q, at, 0:seg] = t[0:rows, q * seg : (q + 1) * seg]
            tb[zz, q, at, seg : 2 * seg] = t[rows : 2 * rows, q * seg : (q + 1) * seg]
        cb[zz, p, at] = tb[zz, p, at]

        def send(e, carry):
            q = lax.rem(p + e, NP)
            remote(tb.at[zz, q, at], cb.at[zz, p, at], tx_s, tx_r.at[zz], {"fsdp": z * NP + q}).start()
            return carry

        lax.fori_loop(1, NP, send, 0)

    def turn(i, carry):
        zz = order(i)

        @pl.when(i > 0)
        def _():
            wait(pr.at[zz], pz_r.at[zz])

        turn_rows(zz, 0, row)
        return carry

    def turn_last(h, carry):
        half = row // 2
        wait(pr.at[0, :, pl.ds(0, half)], pl_r.at[h])
        turn_rows(up(z, -LAST, NZ), pl.multiple_of(h * half, half), half)
        return carry

    lax.fori_loop(0, 3, turn, 0)
    left_pass(last)
    left_share(two)
    lax.fori_loop(3, 5, turn, 0)

    def transpose(i, carry):
        planes = pl.ds(i * 2, 2)
        rt[:, pl.ds(pl.multiple_of(i * 2 * NP * rb.shape[3], 2 * NP * rb.shape[3]), 2 * NP * rb.shape[3])] = (
            rb[planes].reshape(2 * NP * rb.shape[3], width).T
        )
        return carry

    lax.fori_loop(0, NZ // 2, transpose, 0)
    left_share(last)
    lax.fori_loop(5, 7, turn, 0)
    lax.fori_loop(0, 2, turn_last, 0)

    def left_done(zz, carry):
        left_core(zz).wait_recv()
        return carry

    lax.fori_loop(0, NZ, left_done, 0)
    seg = width // NP
    part = width // 4

    def project(i, carry):
        zz = order(i)
        l, q = zz // 4, lax.rem(zz, 4)
        wait(cb.at[zz, pl.ds(0, NP - 1)], tx_r.at[zz])
        turned = cb[zz].reshape(NP * row, 2 * seg)
        for k in range(4):
            at = slice(k * part, (k + 1) * part)
            basis = lb[l, pl.ds(2 * q, 2), :, :, :, at].reshape(NP * row, part)
            ac[l, at] += lax.dot_general(basis, turned, (((0,), (0,)), ((), ())), preferred_element_type=F32)
        return carry

    lax.fori_loop(0, NZ, project, 0)
    loads[4].wait()

    def scale(l):
        def piece(i, carry):
            inside = pl.ds(pl.multiple_of(i * part, part), part)
            rows = pl.ds(pl.multiple_of(l * width + i * part, part), part)
            g, m = ac[l, inside, :seg], ac[l, inside, seg:]
            s = BETA_TWO * sv[rows, :] + (1.0 - BETA_TWO) * g * g
            sv[rows, :] = s
            sc[rows, :] = (m / (jnp.sqrt(s) + EPSILON)).astype(BF16)
            return carry

        lax.fori_loop(0, 4, piece, 0)

    def far(i):
        zz = z
        for step, d in enumerate(RETURN):
            zz = jnp.where(i == step, up(z, d, NZ), zz)
        return zz

    def back(i, carry):
        zz = far(i)
        l, q = zz // 4, lax.rem(zz, 4)
        basis = lb[l, pl.ds(2 * q, 2)].reshape(NP * row, width)
        scaled = sc[pl.ds(pl.multiple_of(l * width, width), width), :]
        out = jnp.dot(basis, scaled, preferred_element_type=F32).astype(BF16)
        bk[zz] = out.reshape(NP, row, seg)
        wb[zz, p] = bk[zz, p]

        def send(e, carry):
            q = lax.rem(p + e, NP)
            remote(bk.at[zz, q], wb.at[zz, p], bx_s, bx_r.at[zz], {"fsdp": z * NP + q}).start()
            return carry

        lax.fori_loop(1, NP, send, 0)
        return carry

    first = up(z, RETURN[0], NZ) // 4
    scale(first)
    lax.fori_loop(0, 1, back, 0)
    scale(1 - first)
    store_s = pltpu.make_async_copy(sv, sec_o, out_sem.at[1])
    store_s.start()
    lax.fori_loop(1, NZ, back, 0)

    mine = pl.ds(pl.multiple_of(z * width, width), width)

    def update(i, carry):
        zz = far(i)
        wait(wb.at[zz, pl.ds(0, NP - 1)], bx_r.at[zz])
        rows = jnp.concatenate([wb[zz, q] for q in range(NP)], axis=1)
        out = jnp.dot(rows, rt[...], preferred_element_type=F32)
        ub[zz] = out.astype(BF16)

        @pl.when(i < NZ - 1)
        def _():
            remote(ub.at[zz], upd_o.at[:, mine], uz_s, uz_r, dev(zz, x, c)).start()

        return carry

    lax.fori_loop(0, NZ, update, 0)
    store_u = pltpu.make_async_copy(ub.at[z], upd_o.at[:, mine], out_sem.at[2])
    store_u.start()

    for way in range(2):
        wait(rb.at[:, x, c], rx_s.at[way])
        right_half(way).wait_send()
        for step in range(4):
            left_z(step, way).wait_send()
    for i in range(4):
        right_core(x, i).wait_send()

    def drain(zz, carry):
        for way in range(2):
            left_x(zz, way).wait_send()
            left_half(zz, way).wait_send()
        left_core(zz).wait_send()
        return carry

    lax.fori_loop(0, NZ, drain, 0)
    wait(right.at[pl.ds(0, NZ - 1)], rz_s)
    wait(ps.at[pl.ds(0, NZ - 1)], pz_s)
    wait(tb.at[pl.ds(0, NZ - 1)], tx_s)
    wait(bk.at[pl.ds(0, NZ - 1)], bx_s)
    wait(ub.at[pl.ds(0, NZ - 1)], uz_s)
    wait(ub.at[pl.ds(0, NZ - 1)], uz_r)
    store_m.wait()
    store_s.wait()
    store_u.wait()


def finish(update, mom, sec, upd_o, mom_o, sec_o, ub, uf, sem):
    parts = 4
    step = uf.shape[1] // parts
    cols = [pl.ds(i * step, step) for i in range(parts)]
    loads = [pltpu.make_async_copy(update.at[:, at], ub.at[:, at], sem.at[i]) for i, at in enumerate(cols)]
    stores = [pltpu.make_async_copy(mom, mom_o, sem.at[parts]), pltpu.make_async_copy(sec, sec_o, sem.at[parts + 1])]
    for copy in loads + stores:
        copy.start()
    for i, at in enumerate(cols):
        loads[i].wait()
        uf[:, at] = ub[:, at].astype(F32)
        stores.append(pltpu.make_async_copy(uf.at[:, at], upd_o.at[:, at], sem.at[parts + 2 + i]))
        stores[-1].start()
    for store in stores:
        store.wait()


def local(grad, moment, second, left_basis, right_basis):
    row, cols = grad.shape
    lblocks, piece, width = left_basis.shape
    total, seg = second.shape
    any_spec = pl.BlockSpec(memory_space=pl.ANY)
    dma = pltpu.SemaphoreType.DMA
    update, moment_new, second_new = pl.pallas_call(
        kernel,
        out_shape=(pltpu.VMEM((row, cols), BF16), pltpu.VMEM((row, cols), F32), pltpu.VMEM((total, seg), F32)),
        in_specs=[any_spec] * 5,
        out_specs=[any_spec] * 3,
        scratch_shapes=[
            pltpu.VMEM((row, cols), F32),
            pltpu.VMEM((row, cols), F32),
            pltpu.VMEM((total, seg), F32),
            pltpu.VMEM((NZ, 2, row, width), BF16),
            pltpu.VMEM((NZ, 2, row, width), BF16),
            pltpu.VMEM((NZ, NX, NC, piece, width), BF16),
            pltpu.VMEM((width, width), BF16),
            pltpu.VMEM((NZ, NP, row, 2 * seg), BF16),
            pltpu.VMEM((NZ, NP, row, 2 * seg), BF16),
            pltpu.VMEM((lblocks, NZ, NX, NC, piece, width), BF16),
            pltpu.VMEM((lblocks, width, 2 * seg), F32),
            pltpu.VMEM((total, seg), BF16),
            pltpu.VMEM((NZ, NP, row, seg), BF16),
            pltpu.VMEM((NZ, NP, row, seg), BF16),
            pltpu.VMEM((NZ, row, width), BF16),
            pltpu.SemaphoreType.REGULAR((NZ // 2 - 1, 2)), dma((5,)), dma((3,)),
            dma, dma((2,)), dma((4,)), dma((4,)), dma((4,)), dma((4,)),
            dma((4, 2)), dma((4, 2)), dma((NZ, 2)), dma((NZ, 2)), dma((NZ, 2)), dma((NZ, 2)), dma((NZ,)), dma((NZ,)),
            dma, dma((NZ,)), dma((2,)), dma, dma((NZ,)), dma, dma((NZ,)), dma, dma,
        ],
        compiler_params=pltpu.CompilerParams(
            collective_id=0, has_side_effects=True, vmem_limit_bytes=61 * 2**20 + 2**18
        ),
        cost_estimate=pl.CostEstimate(flops=3 * 2**30, bytes_accessed=8 * 2**20, transcendentals=2**19),
        name="soap_step",
    )(grad, moment, second, left_basis, right_basis)
    return pl.pallas_call(
        finish,
        out_shape=(
            jax.ShapeDtypeStruct((row, cols), F32),
            jax.ShapeDtypeStruct((row, cols), F32),
            jax.ShapeDtypeStruct((total, seg), F32),
        ),
        in_specs=[any_spec] * 3,
        out_specs=[pl.BlockSpec(memory_space=pltpu.MemorySpace.HBM)] * 3,
        scratch_shapes=[pltpu.VMEM((row, cols), BF16), pltpu.VMEM((row, cols), F32), dma((10,))],
        compiler_params=pltpu.CompilerParams(vmem_limit_bytes=16 * 2**20),
        name="finish",
    )(update, moment_new, second_new)


def solution(mesh):
    in_specs = (
        P(("dp", "fsdp"), None),
        P(("dp", "fsdp"), None),
        P("dp", "fsdp"),
        P("dp", "fsdp", None),
        P("dp", "fsdp", None),
    )
    out_specs = (P(("dp", "fsdp"), None), P(("dp", "fsdp"), None), P("dp", "fsdp"))
    return jax.shard_map(local, mesh=mesh, in_specs=in_specs, out_specs=out_specs, check_vma=False)
```

```python
import jax
import jax.numpy as jnp
from jax import lax
from jax.experimental import pallas as pl
from jax.experimental.pallas import tpu as pltpu
from jax.sharding import PartitionSpec as P

BETA_ONE = 0.9
BETA_TWO = 0.95
EPSILON = 1e-08

NZ, NX, NC = 8, 4, 2
NP = NX * NC
F32, BF16 = jnp.float32, jnp.bfloat16

FILL = (1, -1)
REST = (2, -2, 3, -3, 4)
LAST = REST[-1]

RETURN = (3, -3, 2, -2, 4, 1, -1)


def kernel(
    grad, moment, second, left, right,
    upd_o, mom_o, sec_o,
    gv, mv, sv, ps, pr, rb, rt, tb, cb, lb, ac, sc, bk, wb, ub,
    here, in_sem, out_sem,
    rz_s, rz_r, rx_s, rx_r, rd_s, rd_r,
    lz_s, lz_r, lx_s, lx_r, lo_s, lo_r, ld_s, ld_r,
    pz_s, pz_r, pl_r, tx_s, tx_r, bx_s, bx_r, uz_s, uz_r,
):
    f = lax.axis_index("fsdp")
    z, p = f // NP, lax.rem(f, NP)
    x, c = p // NC, lax.rem(p, NC)
    row = gv.shape[0]
    width = rb.shape[-1]

    def dev(zz, xx, cc):
        return {"fsdp": (zz * NX + xx) * NC + cc}

    def up(v, d, n):
        return lax.rem(v + d + 2 * n, n)

    def zdev(d):
        return dev(up(z, d, NZ), x, c)

    def xdev(d):
        return dev(z, up(x, d, NX), c)

    other = dev(z, x, 1 - c)

    def remote(src, dst, ss, rs, to):
        return pltpu.make_async_remote_copy(
            src_ref=src, dst_ref=dst, send_sem=ss, recv_sem=rs, device_id=to, device_id_type=pl.DeviceIdType.MESH
        )

    def wait(ref, sem):
        pltpu.make_async_copy(ref, ref, sem).wait()

    barrier = pltpu.get_barrier_semaphore()
    for d in (1, -1):
        pl.semaphore_signal(barrier, inc=1, device_id=zdev(d), device_id_type=pl.DeviceIdType.MESH)
    for d in range(1, NP):
        to = {"fsdp": z * NP + lax.rem(p + d, NP)}
        pl.semaphore_signal(barrier, inc=1, device_id=to, device_id_type=pl.DeviceIdType.MESH)

    loads = [
        pltpu.make_async_copy(left, lb.at[:, z, x, c], in_sem.at[0]),
        pltpu.make_async_copy(right.at[z], rb.at[z, x, c], in_sem.at[1]),
        pltpu.make_async_copy(grad, gv, in_sem.at[2]),
        pltpu.make_async_copy(moment, mv, in_sem.at[3]),
        pltpu.make_async_copy(second, sv, in_sem.at[4]),
    ]
    for load in loads:
        load.start()
    ac[...] = jnp.zeros_like(ac)
    loads[0].wait()
    loads[1].wait()
    pl.semaphore_wait(barrier, 2 + NP - 1)

    def right_z(d):
        group = 0 if abs(d) <= 2 else 1
        remote(right.at[up(z, d, NZ)], rb.at[z, x, c], rz_s, rz_r.at[group], zdev(d)).start()

    def left_z(step, way):
        sign = 1 if way == 0 else -1
        blk = up(z, -(0, 1, 2, 2)[step] * sign, NZ)
        ref = lb.at[way, blk, x, c] if step == 3 else lb.at[:, blk, x, c]
        return remote(ref, ref, lz_s.at[step, way], lz_r.at[step, way], zdev((1, 1, 1, 2)[step] * sign))

    def packed_z(d):
        k = up(z, d, NZ)
        if d != LAST:
            remote(ps.at[k], pr.at[z], pz_s, pz_r.at[z], dev(k, x, c)).start()
            return
        for h in range(2):
            rows = pl.ds(h * (row // 2), row // 2)
            remote(ps.at[k, :, rows], pr.at[z, :, rows], pz_s, pl_r.at[h], dev(k, x, c)).start()

    def right_x(zz):
        ref = rb.at[zz, x, c]
        for way in range(2):
            remote(ref, ref, rx_s.at[way], rx_r.at[way], xdev(1 if way == 0 else -1)).start()

    def right_half(way):
        ref = rb.at[pl.ds(way * (NZ // 2), NZ // 2), up(x, -1 if way == 0 else 1, NX), c]
        return remote(ref, ref, rx_s.at[2 + way], rx_r.at[2 + way], xdev(1 if way == 0 else -1))

    def right_core(xx, i):
        ref = rb.at[:, xx, c]
        return remote(ref, ref, rd_s.at[i], rd_r.at[i], other)

    def left_x(zz, way):
        ref = lb.at[:, zz, x, c]
        return remote(ref, ref, lx_s.at[zz, way], lx_r.at[zz, way], xdev(1 if way == 0 else -1))

    def left_half(zz, way):
        ref = lb.at[way, zz, up(x, -1 if way == 0 else 1, NX), c]
        return remote(ref, ref, lo_s.at[zz, way], lo_r.at[zz, way], xdev(1 if way == 0 else -1))

    def left_core(zz):
        ref = lb.at[:, zz, :, c]
        return remote(ref, ref, ld_s.at[zz], ld_r.at[zz], other)

    def near(d):
        return [up(z, -d, NZ), up(z, d, NZ)]

    def left_opposite(way):
        ref = lb.at[way, z, x, c]
        return remote(ref, ref, lo_s.at[z, way], lo_r.at[z, way], xdev(2))

    def left_send(group):
        for zz in group:
            for way in range(2):
                left_x(zz, way).start()

    def left_pass(group):
        for zz in group:
            for way in range(2):
                left_x(zz, way).wait_recv()
                left_half(zz, way).start()

    def left_share(group):
        for zz in group:
            for way in range(2):
                left_half(zz, way).wait_recv()
            left_core(zz).start()

    own, two, last = [z], near(2), near(3) + [up(z, 4, NZ)]

    for way in range(2):
        left_z(0, way).start()
    left_send(own)
    right_x(z)
    for way in range(2):
        left_opposite(way).start()
    for d in (1, -1):
        right_z(d)

    for s in range(1, NZ // 2):
        ways = range(2) if s < NZ // 2 - 1 else range(1)
        for way in ways:
            to = zdev(1 if way == 0 else -1)
            pl.semaphore_signal(here.at[s - 1, way], inc=1, device_id=to, device_id_type=pl.DeviceIdType.MESH)
        for way in ways:
            pl.semaphore_wait(here.at[s - 1, way], 1)
        for way in ways:
            right_z(s + 1 if way == 0 else -s - 1)

    loads[2].wait()
    loads[3].wait()

    def pack(k, carry):
        cols = pl.ds(pl.multiple_of(k * width, width), width)
        g = gv[:, cols]
        m = BETA_ONE * mv[:, cols] + (1.0 - BETA_ONE) * g
        mv[:, cols] = m
        ps[k, 0] = g.astype(BF16)
        ps[k, 1] = m.astype(BF16)
        return carry

    lax.fori_loop(0, NZ, pack, 0)
    store_m = pltpu.make_async_copy(mv, mom_o, out_sem.at[0])
    store_m.start()
    pr[z] = ps[z]

    for way in range(2):
        left_z(0, way).wait_recv()
        left_z(1, way).start()
    for d in FILL:
        packed_z(d)
    left_send(near(1))

    wait(right.at[pl.ds(0, 4)], rz_r.at[0])
    for zz in near(1) + near(2):
        right_x(zz)
    left_pass(near(1))
    wait(right.at[pl.ds(0, 3)], rz_r.at[1])
    for zz in near(3) + [up(z, 4, NZ)]:
        right_x(zz)

    for way in range(2):
        left_z(1, way).wait_recv()
        left_z(2, way).start()
        left_z(3, way).start()
    for d in REST:
        packed_z(d)
    left_send(two)
    for way in range(2):
        left_x(z, way).wait_recv()
    left_share(own)

    right_core(x, 0).start()
    for way in range(2):
        wait(rb.at[:, x, c], rx_r.at[way])
        right_half(way).start()
        right_core(up(x, -1 if way == 0 else 1, NX), 1 + way).start()

    for way in range(2):
        left_z(2, way).wait_recv()
    left_send(near(3))
    left_pass(two)
    left_share(near(1))
    for way in range(2):
        left_z(3, way).wait_recv()
    left_send([up(z, 4, NZ)])

    for way in range(2):
        right_half(way).wait_recv()
    right_core(up(x, 2, NX), 3).start()
    for i in range(4):
        right_core(x, i).wait_recv()

    def order(i):
        d = z
        for step, other_d in enumerate(FILL + REST):
            d = jnp.where(i == step + 1, up(z, -other_d, NZ), d)
        return d

    def turn_rows(zz, h0, rows):
        at = pl.ds(h0, rows)
        both = pr[zz, :, at].reshape(2 * rows, width)
        t = jnp.dot(both, rb[...].reshape(width, width), preferred_element_type=F32).astype(BF16)
        seg = width // NP
        for q in range(NP):
            tb[zz, q, at, 0:seg] = t[0:rows, q * seg : (q + 1) * seg]
            tb[zz, q, at, seg : 2 * seg] = t[rows : 2 * rows, q * seg : (q + 1) * seg]
        cb[zz, p, at] = tb[zz, p, at]

        def send(e, carry):
            q = lax.rem(p + 1 + lax.rem(e + 2, NP - 1), NP)
            remote(tb.at[zz, q, at], cb.at[zz, p, at], tx_s, tx_r.at[zz], {"fsdp": z * NP + q}).start()
            return carry

        lax.fori_loop(1, NP, send, 0)

    def turn(i, carry):
        zz = order(i)

        @pl.when(i > 0)
        def _():
            wait(pr.at[zz], pz_r.at[zz])

        turn_rows(zz, 0, row)
        return carry

    def turn_last(h, carry):
        half = row // 2
        wait(pr.at[0, :, pl.ds(0, half)], pl_r.at[h])
        turn_rows(up(z, -LAST, NZ), pl.multiple_of(h * half, half), half)
        return carry

    lax.fori_loop(0, 3, turn, 0)
    left_pass(last)
    left_share(two)
    lax.fori_loop(3, 5, turn, 0)

    def transpose(i, carry):
        planes = pl.ds(i * 2, 2)
        rt[:, pl.ds(pl.multiple_of(i * 2 * NP * rb.shape[3], 2 * NP * rb.shape[3]), 2 * NP * rb.shape[3])] = (
            rb[planes].reshape(2 * NP * rb.shape[3], width).T
        )
        return carry

    lax.fori_loop(0, NZ // 2, transpose, 0)
    left_share(last)
    lax.fori_loop(5, 7, turn, 0)
    lax.fori_loop(0, 2, turn_last, 0)

    def left_done(zz, carry):
        left_core(zz).wait_recv()
        return carry

    lax.fori_loop(0, NZ, left_done, 0)
    seg = width // NP
    part = width // 4

    def project(i, carry):
        zz = order(i)
        l, q = zz // 4, lax.rem(zz, 4)
        wait(cb.at[zz, pl.ds(0, NP - 1)], tx_r.at[zz])
        turned = cb[zz].reshape(NP * row, 2 * seg)
        for k in range(4):
            at = slice(k * part, (k + 1) * part)
            basis = lb[l, pl.ds(2 * q, 2), :, :, :, at].reshape(NP * row, part)
            ac[l, at] += lax.dot_general(basis, turned, (((0,), (0,)), ((), ())), preferred_element_type=F32)
        return carry

    lax.fori_loop(0, NZ, project, 0)
    loads[4].wait()

    def scale(l):
        def piece(i, carry):
            inside = pl.ds(pl.multiple_of(i * part, part), part)
            rows = pl.ds(pl.multiple_of(l * width + i * part, part), part)
            g, m = ac[l, inside, :seg], ac[l, inside, seg:]
            s = BETA_TWO * sv[rows, :] + (1.0 - BETA_TWO) * g * g
            sv[rows, :] = s
            sc[rows, :] = (m / (jnp.sqrt(s) + EPSILON)).astype(BF16)
            return carry

        lax.fori_loop(0, 4, piece, 0)

    def far(i):
        zz = z
        for step, d in enumerate(RETURN):
            zz = jnp.where(i == step, up(z, d, NZ), zz)
        return zz

    def back(i, carry):
        zz = far(i)
        l, q = zz // 4, lax.rem(zz, 4)
        basis = lb[l, pl.ds(2 * q, 2)].reshape(NP * row, width)
        scaled = sc[pl.ds(pl.multiple_of(l * width, width), width), :]
        out = jnp.dot(basis, scaled, preferred_element_type=F32).astype(BF16)
        bk[zz] = out.reshape(NP, row, seg)
        wb[zz, p] = bk[zz, p]

        def send(e, carry):
            q = lax.rem(p + 1 + lax.rem(e + 2, NP - 1), NP)
            remote(bk.at[zz, q], wb.at[zz, p], bx_s, bx_r.at[zz], {"fsdp": z * NP + q}).start()
            return carry

        lax.fori_loop(1, NP, send, 0)
        return carry

    first = up(z, RETURN[0], NZ) // 4
    scale(first)
    lax.fori_loop(0, 1, back, 0)
    scale(1 - first)
    store_s = pltpu.make_async_copy(sv, sec_o, out_sem.at[1])
    store_s.start()
    lax.fori_loop(1, NZ, back, 0)

    mine = pl.ds(pl.multiple_of(z * width, width), width)

    def update(i, carry):
        zz = far(i)
        wait(wb.at[zz, pl.ds(0, NP - 1)], bx_r.at[zz])
        rows = jnp.concatenate([wb[zz, q] for q in range(NP)], axis=1)
        out = jnp.dot(rows, rt[...], preferred_element_type=F32)
        ub[zz] = out.astype(BF16)

        @pl.when(i < NZ - 1)
        def _():
            remote(ub.at[zz], upd_o.at[:, mine], uz_s, uz_r, dev(zz, x, c)).start()

        return carry

    lax.fori_loop(0, NZ, update, 0)
    store_u = pltpu.make_async_copy(ub.at[z], upd_o.at[:, mine], out_sem.at[2])
    store_u.start()

    for way in range(2):
        wait(rb.at[:, x, c], rx_s.at[way])
        right_half(way).wait_send()
        for step in range(4):
            left_z(step, way).wait_send()
    for i in range(4):
        right_core(x, i).wait_send()

    def drain(zz, carry):
        for way in range(2):
            left_x(zz, way).wait_send()
            left_half(zz, way).wait_send()
        left_core(zz).wait_send()
        return carry

    lax.fori_loop(0, NZ, drain, 0)
    wait(right.at[pl.ds(0, NZ - 1)], rz_s)
    wait(ps.at[pl.ds(0, NZ - 1)], pz_s)
    wait(tb.at[pl.ds(0, NZ - 1)], tx_s)
    wait(bk.at[pl.ds(0, NZ - 1)], bx_s)
    wait(ub.at[pl.ds(0, NZ - 1)], uz_s)
    wait(ub.at[pl.ds(0, NZ - 1)], uz_r)
    store_m.wait()
    store_s.wait()
    store_u.wait()


def finish(update, mom, sec, upd_o, mom_o, sec_o, ub, uf, sem):
    parts = 4
    step = uf.shape[1] // parts
    cols = [pl.ds(i * step, step) for i in range(parts)]
    loads = [pltpu.make_async_copy(update.at[:, at], ub.at[:, at], sem.at[i]) for i, at in enumerate(cols)]
    stores = [pltpu.make_async_copy(mom, mom_o, sem.at[parts]), pltpu.make_async_copy(sec, sec_o, sem.at[parts + 1])]
    for copy in loads + stores:
        copy.start()
    for i, at in enumerate(cols):
        loads[i].wait()
        uf[:, at] = ub[:, at].astype(F32)
        stores.append(pltpu.make_async_copy(uf.at[:, at], upd_o.at[:, at], sem.at[parts + 2 + i]))
        stores[-1].start()
    for store in stores:
        store.wait()


def local(grad, moment, second, left_basis, right_basis):
    row, cols = grad.shape
    lblocks, piece, width = left_basis.shape
    total, seg = second.shape
    any_spec = pl.BlockSpec(memory_space=pl.ANY)
    dma = pltpu.SemaphoreType.DMA
    update, moment_new, second_new = pl.pallas_call(
        kernel,
        out_shape=(pltpu.VMEM((row, cols), BF16), pltpu.VMEM((row, cols), F32), pltpu.VMEM((total, seg), F32)),
        in_specs=[any_spec] * 5,
        out_specs=[any_spec] * 3,
        scratch_shapes=[
            pltpu.VMEM((row, cols), F32),
            pltpu.VMEM((row, cols), F32),
            pltpu.VMEM((total, seg), F32),
            pltpu.VMEM((NZ, 2, row, width), BF16),
            pltpu.VMEM((NZ, 2, row, width), BF16),
            pltpu.VMEM((NZ, NX, NC, piece, width), BF16),
            pltpu.VMEM((width, width), BF16),
            pltpu.VMEM((NZ, NP, row, 2 * seg), BF16),
            pltpu.VMEM((NZ, NP, row, 2 * seg), BF16),
            pltpu.VMEM((lblocks, NZ, NX, NC, piece, width), BF16),
            pltpu.VMEM((lblocks, width, 2 * seg), F32),
            pltpu.VMEM((total, seg), BF16),
            pltpu.VMEM((NZ, NP, row, seg), BF16),
            pltpu.VMEM((NZ, NP, row, seg), BF16),
            pltpu.VMEM((NZ, row, width), BF16),
            pltpu.SemaphoreType.REGULAR((NZ // 2 - 1, 2)), dma((5,)), dma((3,)),
            dma, dma((2,)), dma((4,)), dma((4,)), dma((4,)), dma((4,)),
            dma((4, 2)), dma((4, 2)), dma((NZ, 2)), dma((NZ, 2)), dma((NZ, 2)), dma((NZ, 2)), dma((NZ,)), dma((NZ,)),
            dma, dma((NZ,)), dma((2,)), dma, dma((NZ,)), dma, dma((NZ,)), dma, dma,
        ],
        compiler_params=pltpu.CompilerParams(
            collective_id=0, has_side_effects=True, vmem_limit_bytes=61 * 2**20 + 2**18
        ),
        cost_estimate=pl.CostEstimate(flops=3 * 2**30, bytes_accessed=8 * 2**20, transcendentals=2**19),
        name="soap_step",
    )(grad, moment, second, left_basis, right_basis)
    return pl.pallas_call(
        finish,
        out_shape=(
            jax.ShapeDtypeStruct((row, cols), F32),
            jax.ShapeDtypeStruct((row, cols), F32),
            jax.ShapeDtypeStruct((total, seg), F32),
        ),
        in_specs=[any_spec] * 3,
        out_specs=[pl.BlockSpec(memory_space=pltpu.MemorySpace.HBM)] * 3,
        scratch_shapes=[pltpu.VMEM((row, cols), BF16), pltpu.VMEM((row, cols), F32), dma((10,))],
        compiler_params=pltpu.CompilerParams(vmem_limit_bytes=16 * 2**20),
        name="finish",
    )(update, moment_new, second_new)


def solution(mesh):
    in_specs = (
        P(("dp", "fsdp"), None),
        P(("dp", "fsdp"), None),
        P("dp", "fsdp"),
        P("dp", "fsdp", None),
        P("dp", "fsdp", None),
    )
    out_specs = (P(("dp", "fsdp"), None), P(("dp", "fsdp"), None), P("dp", "fsdp"))
    return jax.shard_map(local, mesh=mesh, in_specs=in_specs, out_specs=out_specs, check_vma=False)
```
